1024 devices in a mesh: gx: 16 (over z), gy: 8 (over x, core), band: 8 (over y).
Axes of the slice: x: 4, y: 8, z: 16, core: 2. Of those that a mesh axis runs over, the one named last changes fastest.
Arguments:
- orbitals: float32 [32, 128, 64, 128], P('band', 'gx', 'gy'), may hold values from -6 to 6
- potential: float32 [128, 64, 128], P('gx', 'gy'), may hold values from -2 to 1
Outputs:
- rotated: float32 [32, 128, 64, 128], P('band', 'gx', 'gy')
The draws below stay inside these ranges and needn't reach their ends.
All inputs are finite; a program needn't handle non-finite values.
Results may differ from the reference program's by a relative error of at most 0.00007.
Values sent between devices are 32-bit elements; how exact they have to be, the bound alone decides.
A program may use at most 32 MiB of HBM per device.

```python
import jax
import jax.numpy as jnp
from jax import lax

NZ = 128
NB = 32
NX = 128
NY = 64


def shard_levels(stream_key, dims, split, smallest, top_value):
    def one(axis_at, blocks):
        heights = jax.random.uniform(jax.random.fold_in(jax.random.fold_in(stream_key, 6), axis_at), (blocks,), jnp.float32, smallest / len(split), top_value / len(split))
        return jnp.repeat(jnp.exp(heights), dims[axis_at] // blocks).reshape((-1,) + (1,) * (len(dims) - axis_at - 1))

    gain = one(*split[0])
    for cut in split[1:]:
        gain = gain * one(*cut)
    return gain


def normal_values(key, shape, spread, bound, split=(), held_as=jnp.bfloat16):
    result = spread * jax.random.normal(key, shape, jnp.float32)
    if split:
        result = result * shard_levels(key, shape, split, -0.22, 0.18)
    return jnp.clip(result, -bound, bound).astype(held_as)


def setup_inputs(seed: int = 0) -> dict:
    key_list = jax.random.split(jax.random.key(seed), 3)
    return {
        "orbitals": normal_values(key_list[0], (NB, NX, NY, NZ), 1.0, 6.0, ((0, 8), (1, 16), (2, 8)), jnp.float32),
        "potential": jnp.clip(-2.0 + 3.0 * jax.random.uniform(key_list[1], (NX, NY, NZ), jnp.float32) ** shard_levels(key_list[1], (NX, NY, NZ), ((0, 16), (1, 8)), -0.2, 0.2), -2.0, 1.0),
    }


COEF = (-5369.0 / 1800.0, 12.0 / 7.0, -15.0 / 56.0, 10.0 / 189.0, -1.0 / 112.0, 2.0 / 1925.0, -1.0 / 16632.0)
LOWER_EDGE = 4.0
UPPER_EDGE = 16.0
BOTTOM_EDGE = -2.5

def hamiltonian(field, potential):
    laplace = 3.0 * COEF[0] * field
    for offset in range(1, 7):
        beside_all = jnp.zeros_like(field)
        for axis_number in range(3):
            beside_all = beside_all + jnp.roll(field, offset, axis_number) + jnp.roll(field, -offset, axis_number)
        laplace = laplace + COEF[offset] * beside_all
    return -0.5 * laplace + potential * field

def filter_one(field, potential):
    half_width = (UPPER_EDGE - LOWER_EDGE) / 2.0
    centre = (UPPER_EDGE + LOWER_EDGE) / 2.0
    sigma_first = half_width / (BOTTOM_EDGE - centre)
    sigma_now = sigma_first
    earlier = field
    current = (hamiltonian(field, potential) - centre * field) * (sigma_first / half_width)
    for order_index in range(2):
        sigma_next = 1.0 / (2.0 / sigma_first - sigma_now)
        latest = 2.0 * sigma_next / half_width * (hamiltonian(current, potential) - centre * current) - sigma_now * sigma_next * earlier
        earlier = current
        current = latest
        sigma_now = sigma_next
    return current

def reference(orbitals, potential):
    filtered = lax.map(lambda one_band: filter_one(one_band, potential), orbitals)
    count = filtered.shape[0]
    flat = filtered.reshape(count, -1)
    intersection = jnp.dot(flat.astype(jnp.float32), flat.T.astype(jnp.float32), precision=lax.Precision.HIGHEST, preferred_element_type=jnp.float32) / float(flat.shape[1])
    lower = jnp.linalg.cholesky(intersection)
    inverse = lax.linalg.triangular_solve(lower, jnp.eye(count, dtype=jnp.float32), left_side=True, lower=True)
    rotated = jnp.dot(inverse.astype(jnp.float32), flat.astype(jnp.float32), precision=lax.Precision.HIGHEST, preferred_element_type=jnp.float32)
    return rotated.reshape(filtered.shape)
```

```python
import functools

import jax
import jax.numpy as jnp
from jax import lax
from jax.experimental import pallas as pl
from jax.experimental.pallas import tpu as pltpu
from jax.sharding import PartitionSpec as P

COEF = (
    -5369.0 / 1800.0,
    12.0 / 7.0,
    -15.0 / 56.0,
    10.0 / 189.0,
    -1.0 / 112.0,
    2.0 / 1925.0,
    -1.0 / 16632.0,
)
LOWER_EDGE = 4.0
UPPER_EDGE = 16.0
BOTTOM_EDGE = -2.5
REACH = 6
MESH = pl.DeviceIdType.MESH


def chebyshev_weights():
    half = (UPPER_EDGE - LOWER_EDGE) / 2.0
    centre = (UPPER_EDGE + LOWER_EDGE) / 2.0
    first = half / (BOTTOM_EDGE - centre)
    rounds = [(first / half, 0.0)]
    now = first
    for _ in range(2):
        following = 1.0 / (2.0 / first - now)
        rounds.append((2.0 * following / half, now * following))
        now = following
    return centre, rounds


CENTRE, ROUNDS = chebyshev_weights()


def split_three(value):
    high = value.astype(jnp.bfloat16)
    rest = value - high.astype(jnp.float32)
    middle = rest.astype(jnp.bfloat16)
    low = (rest - middle.astype(jnp.float32)).astype(jnp.bfloat16)
    return high, middle, low


def kernel(
    sizes, orb_ref, pot_ref, out_ref, xb, yb, acc, fown, fc, rb, ob, sums_gy, sums_band, sums_gx, gram,
    load_sem, x_send, x_recv, y_send, y_recv, a_send, a_recv, b_send, b_recv,
    gy_send, gy_recv, band_send, band_recv, gx_send, gx_recv,
):
    n_gx, n_gy, n_band = sizes
    n_orb, n_x, n_y, n_z = out_ref.shape
    total = n_orb * n_band
    gx = lax.axis_index("gx")
    gy = lax.axis_index("gy")
    band = lax.axis_index("band")
    me = {"gx": gx, "gy": gy, "band": band}
    counts = {"gx": n_gx, "gy": n_gy, "band": n_band}

    def peer(axis, step):
        return lax.rem(me[axis] + step, counts[axis])

    barrier = pltpu.get_barrier_semaphore()
    for axis in ("gx", "gy", "band"):
        @pl.loop(1, counts[axis])
        def _(step, axis=axis):
            pl.semaphore_signal(
                barrier, inc=1, device_id={axis: peer(axis, step)}, device_id_type=MESH
            )

    own_x = pl.ds(REACH, n_x)
    own_y = pl.ds(n_y, n_y)
    load_x = pltpu.make_async_copy(orb_ref, xb.at[0, :, own_x], load_sem.at[0])
    load_y = pltpu.make_async_copy(orb_ref, yb.at[0, :, :, own_y], load_sem.at[1])
    load_x.start()
    load_y.start()
    load_x.wait()
    load_y.wait()
    pl.semaphore_wait(barrier, n_gx + n_gy + n_band - 3)

    def halo(r, o):
        right_x = {"gx": peer("gx", 1)}
        left_x = {"gx": peer("gx", n_gx - 1)}
        right_y = {"gy": peer("gy", 1)}
        left_y = {"gy": peer("gy", n_gy - 1)}

        def move(buf, src, dst, send, recv, target):
            return pltpu.make_async_remote_copy(
                src_ref=buf.at[src], dst_ref=buf.at[dst], send_sem=send, recv_sem=recv,
                device_id=target, device_id_type=MESH,
            )

        every = slice(None)
        return (
            move(xb, (r, o, pl.ds(n_x, REACH)), (r, o, pl.ds(0, REACH)),
                 x_send.at[r, 0, o], x_recv.at[r, 0, o], right_x),
            move(xb, (r, o, pl.ds(REACH, REACH)), (r, o, pl.ds(n_x + REACH, REACH)),
                 x_send.at[r, 1, o], x_recv.at[r, 1, o], left_x),
            move(yb, (r, o, every, pl.ds(2 * n_y - REACH, REACH)),
                 (r, o, every, pl.ds(n_y - REACH, REACH)),
                 y_send.at[r, 0, o], y_recv.at[r, 0, o], right_y),
            move(yb, (r, o, every, pl.ds(n_y, REACH)), (r, o, every, pl.ds(2 * n_y, REACH)),
                 y_send.at[r, 1, o], y_recv.at[r, 1, o], left_y),
        )

    def local_part(r, o):
        scale, back = ROUNDS[r]
        value = xb[r, o, own_x]
        result = scale * ((pot_ref[...] - (1.5 * COEF[0] + CENTRE)) * value)
        if r > 0:
            result = result - back * xb[r - 1, o, own_x]
        flat = value.reshape(n_x * n_y, n_z)
        along_z = jnp.zeros_like(flat)
        for k in range(1, REACH + 1):
            pair = pltpu.roll(flat, k, 1) + pltpu.roll(flat, n_z - k, 1)
            along_z = along_z + (-0.5 * COEF[k] * scale) * pair
        acc[o] = result + along_z.reshape(n_x, n_y, n_z)

    def halo_part(r, o):
        scale = ROUNDS[r][0]
        result = acc[o]
        for k in range(1, REACH + 1):
            pair = xb[r, o, pl.ds(REACH + k, n_x)] + xb[r, o, pl.ds(REACH - k, n_x)]
            pair = pair + yb[r, o, :, pl.ds(n_y + k, n_y)]
            pair = pair + yb[r, o, :, pl.ds(n_y - k, n_y)]
            result = result + (-0.5 * COEF[k] * scale) * pair
        return result

    @pl.loop(0, n_orb)
    def _(o):
        for copy in halo(0, o):
            copy.start()

    @pl.loop(0, n_orb)
    def _(o):
        local_part(0, o)

    for r in range(3):
        @pl.loop(0, n_orb)
        def _(o, r=r):
            for copy in halo(r, o):
                copy.wait_recv()
            result = halo_part(r, o)
            if r < 2:
                xb[r + 1, o, own_x] = result
                yb[r + 1, o, :, own_y] = result
                for copy in halo(r + 1, o):
                    copy.start()
                local_part(r + 1, o)
            else:
                fown[:, pl.ds(pl.multiple_of(o * n_y, n_y), n_y)] = result

    depth = n_orb * n_y

    def rows_of(index):
        return pl.ds(pl.multiple_of(depth * index, depth), depth)

    def spread(source, target):
        return pltpu.make_async_remote_copy(
            src_ref=fown.at[target], dst_ref=fc.at[rows_of(source)],
            send_sem=a_send.at[target], recv_sem=a_recv.at[source],
            device_id={"band": target}, device_id_type=MESH,
        )

    @pl.loop(1, n_band)
    def _(step):
        spread(band, peer("band", step)).start()

    fc[rows_of(band)] = fown[band]

    @pl.loop(1, n_band)
    def _(step):
        spread(peer("band", step), peer("band", step)).wait_recv()

    parts = []
    for y in range(n_y):
        parts.append(split_three(fc[pl.ds(y, total, stride=n_y), :]))
    stacked = jnp.concatenate([jnp.concatenate(part, axis=0) for part in parts], axis=1)
    blocks = lax.dot_general(
        stacked, stacked, (((1,), (1,)), ((), ())), preferred_element_type=jnp.float32
    )
    blocks = blocks[:total] + blocks[total : 2 * total] + blocks[2 * total :]
    gram[:, : 3 * total] = blocks
    gram[:, 3 * total :] = jnp.zeros((total, n_z - 3 * total), jnp.float32)
    wide = gram[...]
    wide = wide + pltpu.roll(wide, n_z - total, 1) + pltpu.roll(wide, n_z - 2 * total, 1)
    lane = lax.broadcasted_iota(jnp.int32, (8, n_z), 1)
    row = lax.broadcasted_iota(jnp.int32, (8, n_z), 0)
    groups = total // 8
    packed = jnp.where(lane < total, wide[:8], 0.0)
    for q in range(1, groups):
        moved = pltpu.roll(wide[8 * q : 8 * q + 8], total * q, 1)
        packed = jnp.where((lane >= total * q) & (lane < total * (q + 1)), moved, packed)

    def sum_over(axis, value, buf, send, recv):
        mine = me[axis]
        buf[mine] = value

        def share(source, target):
            return pltpu.make_async_remote_copy(
                src_ref=buf.at[source], dst_ref=buf.at[source], send_sem=send.at[target],
                recv_sem=recv.at[source], device_id={axis: target}, device_id_type=MESH,
            )

        @pl.loop(1, counts[axis])
        def _(step):
            share(mine, peer(axis, step)).start()

        @pl.loop(1, counts[axis])
        def _(step):
            share(peer(axis, step), peer(axis, step)).wait_recv()

        result = buf[0]
        for index in range(1, counts[axis]):
            result = result + buf[index]
        return result

    packed = sum_over("gy", packed, sums_gy, gy_send, gy_recv)
    packed = sum_over("band", packed, sums_band, band_send, band_recv)
    packed = sum_over("gx", packed, sums_gx, gx_send, gx_recv)
    cells_all = float(n_x * n_y * n_z * n_gx * n_gy)
    packed = packed * (1.0 / cells_all)

    tiles = []
    for q in range(groups):
        tile = packed if q == 0 else pltpu.roll(packed, n_z - total * q, 1)
        eye = jnp.where(lax.rem(lane, total) == row + 8 * q, 1.0, 0.0)
        tiles.append(jnp.where(lane < total, tile, eye))
    for k in range(total):
        home, at = k // 8, k % 8
        pivot_row = tiles[home][at : at + 1, :]
        scaled = pivot_row * (1.0 / pivot_row[:, k : k + 1])
        for q in range(home, groups):
            column = tiles[q][:, k : k + 1]
            if q == home:
                column = jnp.where(row[:, :1] > at, column, 0.0)
            tiles[q] = tiles[q] - column * scaled
    for q in range(groups):
        diagonal = jnp.sum(jnp.where(lane == row + 8 * q, tiles[q], 0.0), axis=1, keepdims=True)
        tiles[q] = jnp.where(lane < total, 0.0, tiles[q] * lax.rsqrt(diagonal))
    inverse = jnp.concatenate(tiles, axis=0)
    lane_all = lax.broadcasted_iota(jnp.int32, (total, n_z), 1)
    high, middle, low = [part.astype(jnp.float32) for part in split_three(inverse)]
    left = jnp.concatenate(
        [
            jnp.where(lane_all < 3 * total, high, middle),
            jnp.where(lane_all < 2 * total, middle, jnp.where(lane_all < 3 * total, high, low)),
        ],
        axis=1,
    ).astype(jnp.bfloat16)
    for y in range(n_y):
        f_high, f_middle, f_low = parts[y]
        right = jnp.concatenate(
            [f_high, f_high, f_middle, f_high, f_high, f_middle, f_low, f_high], axis=0
        )
        rb[pl.ds(y, total, stride=n_y), :] = jnp.dot(
            left, right, preferred_element_type=jnp.float32
        )

    def collect(source, target):
        return pltpu.make_async_remote_copy(
            src_ref=rb.at[rows_of(target)], dst_ref=ob.at[source],
            send_sem=b_send.at[target], recv_sem=b_recv.at[source],
            device_id={"band": target}, device_id_type=MESH,
        )

    @pl.loop(1, n_band)
    def _(step):
        collect(band, peer("band", step)).start()

    ob[band] = rb[rows_of(band)]

    for r in range(3):
        @pl.loop(0, n_orb)
        def _(o, r=r):
            for copy in halo(r, o):
                copy.wait_send()

    @pl.loop(1, n_band)
    def _(step):
        spread(band, peer("band", step)).wait_send()

    for axis, buf, send, recv in (
        ("gy", sums_gy, gy_send, gy_recv),
        ("band", sums_band, band_send, band_recv),
        ("gx", sums_gx, gx_send, gx_recv),
    ):
        @pl.loop(1, counts[axis])
        def _(step, axis=axis, buf=buf, send=send, recv=recv):
            target = peer(axis, step)
            pltpu.make_async_remote_copy(
                src_ref=buf.at[me[axis]], dst_ref=buf.at[me[axis]], send_sem=send.at[target],
                recv_sem=recv.at[me[axis]], device_id={axis: target}, device_id_type=MESH,
            ).wait_send()

    @pl.loop(1, n_band)
    def _(step):
        collect(band, peer("band", step)).wait_send()
        collect(peer("band", step), peer("band", step)).wait_recv()

    for o in range(n_orb):
        out_ref[o] = ob[:, o * n_y : (o + 1) * n_y]


def local(orbitals, potential, sizes):
    n_gx, n_gy, n_band = sizes
    n_orb, n_x, n_y, n_z = orbitals.shape
    total = n_orb * n_band
    f32 = jnp.float32
    dma = pltpu.SemaphoreType.DMA
    vmem = pl.BlockSpec(memory_space=pltpu.VMEM)
    return pl.pallas_call(
        functools.partial(kernel, sizes),
        out_shape=jax.ShapeDtypeStruct(orbitals.shape, f32),
        in_specs=[pl.BlockSpec(memory_space=pl.ANY), vmem],
        out_specs=vmem,
        scratch_shapes=[
            pltpu.VMEM((3, n_orb, n_x + 2 * REACH, n_y, n_z), f32),
            pltpu.VMEM((3, n_orb, n_x, 3 * n_y, n_z), f32),
            pltpu.VMEM((n_orb, n_x, n_y, n_z), f32),
            pltpu.VMEM((n_x, n_orb * n_y, n_z), f32),
            pltpu.VMEM((total * n_y, n_z), f32),
            pltpu.VMEM((total * n_y, n_z), f32),
            pltpu.VMEM((n_x, n_orb * n_y, n_z), f32),
            pltpu.VMEM((n_gy, 8, n_z), f32),
            pltpu.VMEM((n_band, 8, n_z), f32),
            pltpu.VMEM((n_gx, 8, n_z), f32),
            pltpu.VMEM((total, n_z), f32),
            dma((2,)),
            dma((3, 2, n_orb)), dma((3, 2, n_orb)), dma((3, 2, n_orb)), dma((3, 2, n_orb)),
            dma((n_band,)), dma((n_band,)), dma((n_band,)), dma((n_band,)),
            dma((n_gy,)), dma((n_gy,)), dma((n_band,)), dma((n_band,)),
            dma((n_gx,)), dma((n_gx,)),
        ],
        compiler_params=pltpu.CompilerParams(
            collective_id=0, has_side_effects=True, vmem_limit_bytes=24 * 1024 * 1024
        ),
        cost_estimate=pl.CostEstimate(
            flops=16_000_000, bytes_accessed=4 * 2 * orbitals.size, transcendentals=0
        ),
    )(orbitals, potential)


def solution(mesh):
    sizes = tuple(mesh.shape[axis] for axis in ("gx", "gy", "band"))
    in_specs = (P("band", "gx", "gy", None), P("gx", "gy", None))
    out_specs = P("band", "gx", "gy", None)
    return jax.shard_map(
        functools.partial(local, sizes=sizes),
        mesh=mesh, in_specs=in_specs, out_specs=out_specs, check_vma=False,
    )
```

```python
import functools

import jax
import jax.numpy as jnp
from jax import lax
from jax.experimental import pallas as pl
from jax.experimental.pallas import tpu as pltpu
from jax.sharding import PartitionSpec as P

COEF = (
    -5369.0 / 1800.0,
    12.0 / 7.0,
    -15.0 / 56.0,
    10.0 / 189.0,
    -1.0 / 112.0,
    2.0 / 1925.0,
    -1.0 / 16632.0,
)
LOWER_EDGE = 4.0
UPPER_EDGE = 16.0
BOTTOM_EDGE = -2.5
REACH = 6
MESH = pl.DeviceIdType.MESH


def chebyshev_weights():
    half = (UPPER_EDGE - LOWER_EDGE) / 2.0
    centre = (UPPER_EDGE + LOWER_EDGE) / 2.0
    first = half / (BOTTOM_EDGE - centre)
    rounds = [(first / half, 0.0)]
    now = first
    for _ in range(2):
        following = 1.0 / (2.0 / first - now)
        rounds.append((2.0 * following / half, now * following))
        now = following
    return centre, rounds


CENTRE, ROUNDS = chebyshev_weights()


def split_three(value):
    high = value.astype(jnp.bfloat16)
    rest = value - high.astype(jnp.float32)
    middle = rest.astype(jnp.bfloat16)
    low = (rest - middle.astype(jnp.float32)).astype(jnp.bfloat16)
    return high, middle, low


def kernel(
    sizes, orb_ref, pot_hbm, out_ref, pot_ref, xb, yb, acc, fown, fc, rb, ob, sums_gy, sums_band, sums_gx, gram,
    load_sem, x_send, x_recv, y_send, y_recv, a_send, a_recv, b_send, b_recv,
    gy_send, gy_recv, band_send, band_recv, gx_send, gx_recv,
    near, middle_way, far,
):
    n_gx, n_gy, n_band = sizes
    n_orb, n_x, n_y, n_z = out_ref.shape
    total = n_orb * n_band
    gx = lax.axis_index("gx")
    gy = lax.axis_index("gy")
    band = lax.axis_index("band")
    me = {"gx": gx, "gy": gy, "band": band}
    counts = {"gx": n_gx, "gy": n_gy, "band": n_band}

    def peer(axis, step):
        return lax.rem(me[axis] + step, counts[axis])

    barrier = pltpu.get_barrier_semaphore()

    def greet(semaphore, axis, distance):
        for step in (distance, counts[axis] - distance):
            pl.semaphore_signal(
                semaphore, inc=1, device_id={axis: peer(axis, step)}, device_id_type=MESH
            )

    for axis in ("gx", "gy", "band"):
        greet(barrier, axis, 1)

    own_x = pl.ds(REACH, n_x)
    own_y = pl.ds(n_y, n_y)
    load_x = pltpu.make_async_copy(orb_ref, xb.at[0, :, own_x], load_sem.at[0])
    load_y = pltpu.make_async_copy(orb_ref, yb.at[0, :, :, own_y], load_sem.at[1])
    load_pot = pltpu.make_async_copy(pot_hbm, pot_ref, load_sem.at[2])
    load_x.start()
    load_y.start()
    load_pot.start()
    load_x.wait()
    load_y.wait()
    pl.semaphore_wait(barrier, 6)

    def halo(r, o):
        right_x = {"gx": peer("gx", 1)}
        left_x = {"gx": peer("gx", n_gx - 1)}
        right_y = {"gy": peer("gy", 1)}
        left_y = {"gy": peer("gy", n_gy - 1)}

        def move(buf, src, dst, send, recv, target):
            return pltpu.make_async_remote_copy(
                src_ref=buf.at[src], dst_ref=buf.at[dst], send_sem=send, recv_sem=recv,
                device_id=target, device_id_type=MESH,
            )

        every = slice(None)
        return (
            move(xb, (r, o, pl.ds(n_x, REACH)), (r, o, pl.ds(0, REACH)),
                 x_send.at[r, 0, o], x_recv.at[r, 0, o], right_x),
            move(xb, (r, o, pl.ds(REACH, REACH)), (r, o, pl.ds(n_x + REACH, REACH)),
                 x_send.at[r, 1, o], x_recv.at[r, 1, o], left_x),
            move(yb, (r, o, every, pl.ds(2 * n_y - REACH, REACH)),
                 (r, o, every, pl.ds(n_y - REACH, REACH)),
                 y_send.at[r, 0, o], y_recv.at[r, 0, o], right_y),
            move(yb, (r, o, every, pl.ds(n_y, REACH)), (r, o, every, pl.ds(2 * n_y, REACH)),
                 y_send.at[r, 1, o], y_recv.at[r, 1, o], left_y),
        )

    def local_part(r, o):
        scale, back = ROUNDS[r]
        value = xb[r, o, own_x]
        result = scale * ((pot_ref[...] - (1.5 * COEF[0] + CENTRE)) * value)
        if r > 0:
            result = result - back * xb[r - 1, o, own_x]
        flat = value.reshape(n_x * n_y, n_z)
        along_z = jnp.zeros_like(flat)
        for k in range(1, REACH + 1):
            pair = pltpu.roll(flat, k, 1) + pltpu.roll(flat, n_z - k, 1)
            along_z = along_z + (-0.5 * COEF[k] * scale) * pair
        acc[o] = result + along_z.reshape(n_x, n_y, n_z)

    def halo_part(r, o):
        scale = ROUNDS[r][0]
        result = acc[o]
        for k in range(1, REACH + 1):
            pair = xb[r, o, pl.ds(REACH + k, n_x)] + xb[r, o, pl.ds(REACH - k, n_x)]
            pair = pair + yb[r, o, :, pl.ds(n_y + k, n_y)]
            pair = pair + yb[r, o, :, pl.ds(n_y - k, n_y)]
            result = result + (-0.5 * COEF[k] * scale) * pair
        return result

    @pl.loop(0, n_orb)
    def _(o):
        for copy in halo(0, o):
            copy.start()

    greet(near, "band", 1)
    load_pot.wait()

    @pl.loop(0, n_orb)
    def _(o):
        local_part(0, o)

    depth = n_orb * n_y

    def rows_of(index):
        return pl.ds(pl.multiple_of(depth * index, depth), depth)

    def spread(target, o):
        start = pl.multiple_of(o * n_y, n_y)
        return pltpu.make_async_remote_copy(
            src_ref=fown.at[target, pl.ds(start, n_y)],
            dst_ref=fc.at[pl.ds(pl.multiple_of(depth * band + start, n_y), n_y)],
            send_sem=a_send.at[target], recv_sem=a_recv.at[band],
            device_id={"band": target}, device_id_type=MESH,
        )

    def spread_whole(source, target):
        return pltpu.make_async_remote_copy(
            src_ref=fown.at[target], dst_ref=fc.at[rows_of(source)],
            send_sem=a_send.at[target], recv_sem=a_recv.at[source],
            device_id={"band": target}, device_id_type=MESH,
        )

    def by_distance(count):
        return sorted(range(1, count), key=lambda step: min(step, count - step))

    for r in range(3):
        if r == 1:
            pl.semaphore_wait(near, 2)
            greet(middle_way, "band", 2)
        if r == 2:
            pl.semaphore_wait(middle_way, 2)

        @pl.loop(0, n_orb)
        def _(o, r=r):
            for copy in halo(r, o):
                copy.wait_recv()
            result = halo_part(r, o)
            if r < 2:
                xb[r + 1, o, own_x] = result
                yb[r + 1, o, :, own_y] = result
                for copy in halo(r + 1, o):
                    copy.start()
                local_part(r + 1, o)
            else:
                fown[:, pl.ds(pl.multiple_of(o * n_y, n_y), n_y)] = result
                for step in reversed(by_distance(n_band)):
                    spread(peer("band", step), o).start()

    if n_gx > 8:
        greet(far, "gx", 4)
    fc[rows_of(band)] = fown[band]
    for step in by_distance(n_band):
        spread_whole(peer("band", step), band).wait_recv()

    parts = []
    for y in range(n_y):
        parts.append(split_three(fc[pl.ds(y, total, stride=n_y), :]))
    stacked = jnp.concatenate([jnp.concatenate(part, axis=0) for part in parts], axis=1)
    blocks = lax.dot_general(
        stacked, stacked, (((1,), (1,)), ((), ())), preferred_element_type=jnp.float32
    )
    blocks = blocks[:total] + blocks[total : 2 * total] + blocks[2 * total :]
    gram[:, : 3 * total] = blocks
    gram[:, 3 * total :] = jnp.zeros((total, n_z - 3 * total), jnp.float32)
    wide = gram[...]
    wide = wide + pltpu.roll(wide, n_z - total, 1) + pltpu.roll(wide, n_z - 2 * total, 1)
    lane = lax.broadcasted_iota(jnp.int32, (8, n_z), 1)
    row = lax.broadcasted_iota(jnp.int32, (8, n_z), 0)
    groups = total // 8
    packed = jnp.where(lane < total, wide[:8], 0.0)
    for q in range(1, groups):
        moved = pltpu.roll(wide[8 * q : 8 * q + 8], total * q, 1)
        packed = jnp.where((lane >= total * q) & (lane < total * (q + 1)), moved, packed)

    def sum_over(axis, value, buf, send, recv):
        buf[0] = value

        def share(step):
            return pltpu.make_async_remote_copy(
                src_ref=buf.at[0], dst_ref=buf.at[step], send_sem=send.at[step],
                recv_sem=recv.at[step], device_id={axis: peer(axis, step)}, device_id_type=MESH,
            )

        for step in reversed(by_distance(counts[axis])):
            share(step).start()
        for step in by_distance(counts[axis]):
            share(step).wait_recv()
            value = value + buf[step]
        return value

    packed = sum_over("gy", packed, sums_gy, gy_send, gy_recv)
    packed = sum_over("band", packed, sums_band, band_send, band_recv)
    if n_gx > 8:
        pl.semaphore_wait(far, 2)
    packed = sum_over("gx", packed, sums_gx, gx_send, gx_recv)
    cells_all = float(n_x * n_y * n_z * n_gx * n_gy)
    packed = packed * (1.0 / cells_all)

    tiles = []
    for q in range(groups):
        tile = packed if q == 0 else pltpu.roll(packed, n_z - total * q, 1)
        eye = jnp.where(lax.rem(lane, total) == row + 8 * q, 1.0, 0.0)
        tiles.append(jnp.where(lane < total, tile, eye))
    for k in range(total):
        home, at = k // 8, k % 8
        pivot_row = tiles[home][at : at + 1, :]
        scaled = pivot_row * (1.0 / pivot_row[:, k : k + 1])
        for q in range(home, groups):
            column = tiles[q][:, k : k + 1]
            if q == home:
                column = jnp.where(row[:, :1] > at, column, 0.0)
            tiles[q] = tiles[q] - column * scaled
    for q in range(groups):
        diagonal = jnp.sum(jnp.where(lane == row + 8 * q, tiles[q], 0.0), axis=1, keepdims=True)
        tiles[q] = jnp.where(lane < total, 0.0, tiles[q] * lax.rsqrt(diagonal))
    inverse = jnp.concatenate(tiles, axis=0)
    lane_all = lax.broadcasted_iota(jnp.int32, (total, n_z), 1)
    high, middle, low = [part.astype(jnp.float32) for part in split_three(inverse)]
    left = jnp.concatenate(
        [
            jnp.where(lane_all < 3 * total, high, middle),
            jnp.where(lane_all < 2 * total, middle, jnp.where(lane_all < 3 * total, high, low)),
        ],
        axis=1,
    ).astype(jnp.bfloat16)
    for y in range(n_y):
        f_high, f_middle, f_low = parts[y]
        right = jnp.concatenate(
            [f_high, f_high, f_middle, f_high, f_high, f_middle, f_low, f_high], axis=0
        )
        rb[pl.ds(y, total, stride=n_y), :] = jnp.dot(
            left, right, preferred_element_type=jnp.float32
        )

    def collect(source, target):
        return pltpu.make_async_remote_copy(
            src_ref=rb.at[rows_of(target)], dst_ref=ob.at[source],
            send_sem=b_send.at[target], recv_sem=b_recv.at[source],
            device_id={"band": target}, device_id_type=MESH,
        )

    for step in reversed(by_distance(n_band)):
        collect(band, peer("band", step)).start()

    ob[band] = rb[rows_of(band)]

    for r in range(3):
        @pl.loop(0, n_orb)
        def _(o, r=r):
            for copy in halo(r, o):
                copy.wait_send()

    @pl.loop(1, n_band)
    def _(step):
        spread_whole(band, peer("band", step)).wait_send()

    for axis, buf, send, recv in (
        ("gy", sums_gy, gy_send, gy_recv),
        ("band", sums_band, band_send, band_recv),
        ("gx", sums_gx, gx_send, gx_recv),
    ):
        @pl.loop(1, counts[axis])
        def _(step, axis=axis, buf=buf, send=send, recv=recv):
            pltpu.make_async_remote_copy(
                src_ref=buf.at[0], dst_ref=buf.at[step], send_sem=send.at[step],
                recv_sem=recv.at[step], device_id={axis: peer(axis, step)}, device_id_type=MESH,
            ).wait_send()

    @pl.loop(1, n_band)
    def _(step):
        collect(band, peer("band", step)).wait_send()
        collect(peer("band", step), peer("band", step)).wait_recv()

    for o in range(n_orb):
        out_ref[o] = ob[:, o * n_y : (o + 1) * n_y]


def local(orbitals, potential, sizes):
    n_gx, n_gy, n_band = sizes
    n_orb, n_x, n_y, n_z = orbitals.shape
    total = n_orb * n_band
    f32 = jnp.float32
    dma = pltpu.SemaphoreType.DMA
    vmem = pl.BlockSpec(memory_space=pltpu.VMEM)
    return pl.pallas_call(
        functools.partial(kernel, sizes),
        out_shape=jax.ShapeDtypeStruct(orbitals.shape, f32),
        in_specs=[pl.BlockSpec(memory_space=pl.ANY)] * 2,
        out_specs=vmem,
        scratch_shapes=[
            pltpu.VMEM((n_x, n_y, n_z), f32),
            pltpu.VMEM((3, n_orb, n_x + 2 * REACH, n_y, n_z), f32),
            pltpu.VMEM((3, n_orb, n_x, 3 * n_y, n_z), f32),
            pltpu.VMEM((n_orb, n_x, n_y, n_z), f32),
            pltpu.VMEM((n_x, n_orb * n_y, n_z), f32),
            pltpu.VMEM((total * n_y, n_z), f32),
            pltpu.VMEM((total * n_y, n_z), f32),
            pltpu.VMEM((n_x, n_orb * n_y, n_z), f32),
            pltpu.VMEM((n_gy, 8, n_z), f32),
            pltpu.VMEM((n_band, 8, n_z), f32),
            pltpu.VMEM((n_gx, 8, n_z), f32),
            pltpu.VMEM((total, n_z), f32),
            dma((3,)),
            dma((3, 2, n_orb)), dma((3, 2, n_orb)), dma((3, 2, n_orb)), dma((3, 2, n_orb)),
            dma((n_band,)), dma((n_band,)), dma((n_band,)), dma((n_band,)),
            dma((n_gy,)), dma((n_gy,)), dma((n_band,)), dma((n_band,)),
            dma((n_gx,)), dma((n_gx,)),
            *[pltpu.SemaphoreType.REGULAR] * 3,
        ],
        compiler_params=pltpu.CompilerParams(
            collective_id=0, has_side_effects=True, vmem_limit_bytes=56 * 1024 * 1024
        ),
        cost_estimate=pl.CostEstimate(
            flops=16_000_000, bytes_accessed=4 * 2 * orbitals.size, transcendentals=0
        ),
    )(orbitals, potential)


def solution(mesh):
    sizes = tuple(mesh.shape[axis] for axis in ("gx", "gy", "band"))
    in_specs = (P("band", "gx", "gy", None), P("gx", "gy", None))
    out_specs = P("band", "gx", "gy", None)
    return jax.shard_map(
        functools.partial(local, sizes=sizes),
        mesh=mesh, in_specs=in_specs, out_specs=out_specs, check_vma=False,
    )
```

```python
import functools

import jax
import jax.numpy as jnp
from jax import lax
from jax.experimental import pallas as pl
from jax.experimental.pallas import tpu as pltpu
from jax.sharding import PartitionSpec as P

COEF = (
    -5369.0 / 1800.0,
    12.0 / 7.0,
    -15.0 / 56.0,
    10.0 / 189.0,
    -1.0 / 112.0,
    2.0 / 1925.0,
    -1.0 / 16632.0,
)
LOWER_EDGE = 4.0
UPPER_EDGE = 16.0
BOTTOM_EDGE = -2.5
REACH = 6
MESH = pl.DeviceIdType.MESH


def chebyshev_weights():
    half = (UPPER_EDGE - LOWER_EDGE) / 2.0
    centre = (UPPER_EDGE + LOWER_EDGE) / 2.0
    first = half / (BOTTOM_EDGE - centre)
    rounds = [(first / half, 0.0)]
    now = first
    for _ in range(2):
        following = 1.0 / (2.0 / first - now)
        rounds.append((2.0 * following / half, now * following))
        now = following
    return centre, rounds


CENTRE, ROUNDS = chebyshev_weights()


def split_three(value):
    high = value.astype(jnp.bfloat16)
    rest = value - high.astype(jnp.float32)
    middle = rest.astype(jnp.bfloat16)
    low = (rest - middle.astype(jnp.float32)).astype(jnp.bfloat16)
    return high, middle, low


def kernel(
    sizes, orb_ref, pot_hbm, out_ref, pot_ref, xb, yb, acc, fown, fc, rb, ob, sums_gy, sums_band, sums_gx, gram,
    load_sem, x_send, x_recv, y_send, y_recv, a_send, a_recv, b_send, b_recv,
    gy_send, gy_recv, band_send, band_recv, gx_send, gx_recv,
    near, middle_way, far,
):
    n_gx, n_gy, n_band = sizes
    n_orb, n_x, n_y, n_z = out_ref.shape
    total = n_orb * n_band
    gx = lax.axis_index("gx")
    gy = lax.axis_index("gy")
    band = lax.axis_index("band")
    me = {"gx": gx, "gy": gy, "band": band}
    counts = {"gx": n_gx, "gy": n_gy, "band": n_band}

    def peer(axis, step):
        return lax.rem(me[axis] + step, counts[axis])

    barrier = pltpu.get_barrier_semaphore()

    def greet(semaphore, axis, distance):
        for step in (distance, counts[axis] - distance):
            pl.semaphore_signal(
                semaphore, inc=1, device_id={axis: peer(axis, step)}, device_id_type=MESH
            )

    for axis in ("gx", "gy", "band"):
        greet(barrier, axis, 1)

    own_x = pl.ds(REACH, n_x)
    own_y = pl.ds(n_y, n_y)
    load_x = pltpu.make_async_copy(orb_ref, xb.at[0, :, own_x], load_sem.at[0])
    load_y = pltpu.make_async_copy(orb_ref, yb.at[0, :, :, own_y], load_sem.at[1])
    load_pot = pltpu.make_async_copy(pot_hbm, pot_ref, load_sem.at[2])
    load_x.start()
    load_y.start()
    load_pot.start()
    load_x.wait()
    load_y.wait()
    pl.semaphore_wait(barrier, 6)

    def halo(r, o):
        right_x = {"gx": peer("gx", 1)}
        left_x = {"gx": peer("gx", n_gx - 1)}
        right_y = {"gy": peer("gy", 1)}
        left_y = {"gy": peer("gy", n_gy - 1)}

        def move(buf, src, dst, send, recv, target):
            return pltpu.make_async_remote_copy(
                src_ref=buf.at[src], dst_ref=buf.at[dst], send_sem=send, recv_sem=recv,
                device_id=target, device_id_type=MESH,
            )

        every = slice(None)
        return (
            move(xb, (r, o, pl.ds(n_x, REACH)), (r, o, pl.ds(0, REACH)),
                 x_send.at[r, 0, o], x_recv.at[r, 0, o], right_x),
            move(xb, (r, o, pl.ds(REACH, REACH)), (r, o, pl.ds(n_x + REACH, REACH)),
                 x_send.at[r, 1, o], x_recv.at[r, 1, o], left_x),
            move(yb, (r, o, every, pl.ds(2 * n_y - REACH, REACH)),
                 (r, o, every, pl.ds(n_y - REACH, REACH)),
                 y_send.at[r, 0, o], y_recv.at[r, 0, o], right_y),
            move(yb, (r, o, every, pl.ds(n_y, REACH)), (r, o, every, pl.ds(2 * n_y, REACH)),
                 y_send.at[r, 1, o], y_recv.at[r, 1, o], left_y),
        )

    def local_part(r, o):
        scale, back = ROUNDS[r]
        value = xb[r, o, own_x]
        result = scale * ((pot_ref[...] - (1.5 * COEF[0] + CENTRE)) * value)
        if r > 0:
            result = result - back * xb[r - 1, o, own_x]
        flat = value.reshape(n_x * n_y, n_z)
        along_z = jnp.zeros_like(flat)
        for k in range(1, REACH + 1):
            pair = pltpu.roll(flat, k, 1) + pltpu.roll(flat, n_z - k, 1)
            along_z = along_z + (-0.5 * COEF[k] * scale) * pair
        acc[o] = result + along_z.reshape(n_x, n_y, n_z)

    def halo_part(r, o):
        scale = ROUNDS[r][0]
        result = acc[o]
        for k in range(1, REACH + 1):
            pair = xb[r, o, pl.ds(REACH + k, n_x)] + xb[r, o, pl.ds(REACH - k, n_x)]
            pair = pair + yb[r, o, :, pl.ds(n_y + k, n_y)]
            pair = pair + yb[r, o, :, pl.ds(n_y - k, n_y)]
            result = result + (-0.5 * COEF[k] * scale) * pair
        return result

    @pl.loop(0, n_orb)
    def _(o):
        for copy in halo(0, o):
            copy.start()

    greet(near, "band", 1)
    load_pot.wait()

    @pl.loop(0, n_orb)
    def _(o):
        local_part(0, o)

    depth = n_orb * n_y

    def rows_of(index):
        return pl.ds(pl.multiple_of(depth * index, depth), depth)

    def spread(target, o):
        start = pl.multiple_of(o * n_y, n_y)
        return pltpu.make_async_remote_copy(
            src_ref=fown.at[target, pl.ds(start, n_y)],
            dst_ref=fc.at[pl.ds(pl.multiple_of(depth * band + start, n_y), n_y)],
            send_sem=a_send.at[target], recv_sem=a_recv.at[band],
            device_id={"band": target}, device_id_type=MESH,
        )

    def spread_whole(source, target):
        return pltpu.make_async_remote_copy(
            src_ref=fown.at[target], dst_ref=fc.at[rows_of(source)],
            send_sem=a_send.at[target], recv_sem=a_recv.at[source],
            device_id={"band": target}, device_id_type=MESH,
        )

    def share(step, where, buf, send, recv):
        return pltpu.make_async_remote_copy(
            src_ref=buf.at[0], dst_ref=buf.at[step], send_sem=send.at[step],
            recv_sem=recv.at[step], device_id=where(step), device_id_type=MESH,
        )

    def by_distance(count):
        return sorted(range(1, count), key=lambda step: min(step, count - step))

    other_core = gy + 1 - 2 * lax.rem(gy, 2)
    band_steps = [0] + by_distance(n_band)
    phases = (
        (
            [2 * step + core for step in band_steps for core in (0, 1) if step + core > 0],
            lambda step: {
                "gy": other_core if step % 2 else gy, "band": peer("band", step // 2)
            },
            sums_band, band_send, band_recv,
        ),
        (
            by_distance(n_gy // 2),
            lambda step: {"gy": peer("gy", 2 * step)},
            sums_gy, gy_send, gy_recv,
        ),
        (
            by_distance(n_gx),
            lambda step: {"gx": peer("gx", step)},
            sums_gx, gx_send, gx_recv,
        ),
    )

    for r in range(3):
        if r == 1:
            pl.semaphore_wait(near, 2)
            greet(middle_way, "band", 2)
        if r == 2:
            pl.semaphore_wait(middle_way, 2)

        @pl.loop(0, n_orb)
        def _(o, r=r):
            for copy in halo(r, o):
                copy.wait_recv()
            result = halo_part(r, o)
            if r < 2:
                xb[r + 1, o, own_x] = result
                yb[r + 1, o, :, own_y] = result
                for copy in halo(r + 1, o):
                    copy.start()
                local_part(r + 1, o)
            else:
                fown[:, pl.ds(pl.multiple_of(o * n_y, n_y), n_y)] = result
                for step in reversed(by_distance(n_band)):
                    spread(peer("band", step), o).start()

    if n_gx > 8:
        greet(far, "gx", 4)
    fc[rows_of(band)] = fown[band]
    for step in by_distance(n_band):
        spread_whole(peer("band", step), band).wait_recv()

    parts = []
    for y in range(n_y):
        parts.append(split_three(fc[pl.ds(y, total, stride=n_y), :]))
    stacked = jnp.concatenate([jnp.concatenate(part, axis=0) for part in parts], axis=1)
    blocks = lax.dot_general(
        stacked, stacked, (((1,), (1,)), ((), ())), preferred_element_type=jnp.float32
    )
    blocks = blocks[:total] + blocks[total : 2 * total] + blocks[2 * total :]
    gram[:, : 3 * total] = blocks
    gram[:, 3 * total :] = jnp.zeros((total, n_z - 3 * total), jnp.float32)
    wide = gram[...]
    wide = wide + pltpu.roll(wide, n_z - total, 1) + pltpu.roll(wide, n_z - 2 * total, 1)
    lane = lax.broadcasted_iota(jnp.int32, (8, n_z), 1)
    row = lax.broadcasted_iota(jnp.int32, (8, n_z), 0)
    groups = total // 8
    packed = jnp.where(lane < total, wide[:8], 0.0)
    for q in range(1, groups):
        moved = pltpu.roll(wide[8 * q : 8 * q + 8], total * q, 1)
        packed = jnp.where((lane >= total * q) & (lane < total * (q + 1)), moved, packed)

    def sum_over(steps, where, value, buf, send, recv):
        buf[0] = value
        for step in reversed(steps):
            share(step, where, buf, send, recv).start()
        for step in steps:
            share(step, where, buf, send, recv).wait_recv()
            value = value + buf[step]
        return value

    packed = sum_over(*phases[0][:2], packed, *phases[0][2:])
    packed = sum_over(*phases[1][:2], packed, *phases[1][2:])
    if n_gx > 8:
        pl.semaphore_wait(far, 2)
    packed = sum_over(*phases[2][:2], packed, *phases[2][2:])
    cells_all = float(n_x * n_y * n_z * n_gx * n_gy)
    packed = packed * (1.0 / cells_all)

    tiles = []
    for q in range(groups):
        tile = packed if q == 0 else pltpu.roll(packed, n_z - total * q, 1)
        eye = jnp.where(lax.rem(lane, total) == row + 8 * q, 1.0, 0.0)
        tiles.append(jnp.where(lane < total, tile, eye))
    for home in range(groups):
        columns = [
            [
                jnp.broadcast_to(tiles[q][:, 8 * home + at : 8 * home + at + 1], (8, n_z))
                for q in range(home, groups)
            ]
            for at in range(8)
        ]
        for at in range(8):
            pivot_row = jnp.broadcast_to(tiles[home][at : at + 1, :], (8, n_z))
            reciprocal = 1.0 / jnp.broadcast_to(columns[at][0][at : at + 1, :], (8, n_z))
            factors = [column * reciprocal for column in columns[at]]
            factors[0] = jnp.where(row > at, factors[0], 0.0)
            for factor, q in zip(factors, range(home, groups)):
                tiles[q] = tiles[q] - factor * pivot_row
            for later in range(at + 1, 8):
                value = jnp.broadcast_to(columns[later][0][at : at + 1, :], (8, n_z))
                columns[later] = [
                    column - factor * value for column, factor in zip(columns[later], factors)
                ]
    for q in range(groups):
        diagonal = jnp.sum(jnp.where(lane == row + 8 * q, tiles[q], 0.0), axis=1, keepdims=True)
        tiles[q] = jnp.where(lane < total, 0.0, tiles[q] * lax.rsqrt(diagonal))
    inverse = jnp.concatenate(tiles, axis=0)
    lane_all = lax.broadcasted_iota(jnp.int32, (total, n_z), 1)
    high, middle, low = [part.astype(jnp.float32) for part in split_three(inverse)]
    left = jnp.concatenate(
        [
            jnp.where(lane_all < 3 * total, high, middle),
            jnp.where(lane_all < 2 * total, middle, jnp.where(lane_all < 3 * total, high, low)),
        ],
        axis=1,
    ).astype(jnp.bfloat16)
    for y in range(n_y):
        f_high, f_middle, f_low = parts[y]
        right = jnp.concatenate(
            [f_high, f_high, f_middle, f_high, f_high, f_middle, f_low, f_high], axis=0
        )
        rb[pl.ds(y, total, stride=n_y), :] = jnp.dot(
            left, right, preferred_element_type=jnp.float32
        )

    def collect(source, target):
        return pltpu.make_async_remote_copy(
            src_ref=rb.at[rows_of(target)], dst_ref=ob.at[source],
            send_sem=b_send.at[target], recv_sem=b_recv.at[source],
            device_id={"band": target}, device_id_type=MESH,
        )

    for step in reversed(by_distance(n_band)):
        collect(band, peer("band", step)).start()

    ob[band] = rb[rows_of(band)]

    for r in range(3):
        @pl.loop(0, n_orb)
        def _(o, r=r):
            for copy in halo(r, o):
                copy.wait_send()

    @pl.loop(1, n_band)
    def _(step):
        spread_whole(band, peer("band", step)).wait_send()

    for steps, where, buf, send, recv in phases:
        for step in steps:
            share(step, where, buf, send, recv).wait_send()

    @pl.loop(1, n_band)
    def _(step):
        collect(band, peer("band", step)).wait_send()
        collect(peer("band", step), peer("band", step)).wait_recv()

    for o in range(n_orb):
        out_ref[o] = ob[:, o * n_y : (o + 1) * n_y]


def local(orbitals, potential, sizes):
    n_gx, n_gy, n_band = sizes
    n_orb, n_x, n_y, n_z = orbitals.shape
    total = n_orb * n_band
    f32 = jnp.float32
    dma = pltpu.SemaphoreType.DMA
    vmem = pl.BlockSpec(memory_space=pltpu.VMEM)
    return pl.pallas_call(
        functools.partial(kernel, sizes),
        out_shape=jax.ShapeDtypeStruct(orbitals.shape, f32),
        in_specs=[pl.BlockSpec(memory_space=pl.ANY)] * 2,
        out_specs=vmem,
        scratch_shapes=[
            pltpu.VMEM((n_x, n_y, n_z), f32),
            pltpu.VMEM((3, n_orb, n_x + 2 * REACH, n_y, n_z), f32),
            pltpu.VMEM((3, n_orb, n_x, 3 * n_y, n_z), f32),
            pltpu.VMEM((n_orb, n_x, n_y, n_z), f32),
            pltpu.VMEM((n_x, n_orb * n_y, n_z), f32),
            pltpu.VMEM((total * n_y, n_z), f32),
            pltpu.VMEM((total * n_y, n_z), f32),
            pltpu.VMEM((n_x, n_orb * n_y, n_z), f32),
            pltpu.VMEM((n_gy // 2, 8, n_z), f32),
            pltpu.VMEM((2 * n_band, 8, n_z), f32),
            pltpu.VMEM((n_gx, 8, n_z), f32),
            pltpu.VMEM((total, n_z), f32),
            dma((3,)),
            dma((3, 2, n_orb)), dma((3, 2, n_orb)), dma((3, 2, n_orb)), dma((3, 2, n_orb)),
            dma((n_band,)), dma((n_band,)), dma((n_band,)), dma((n_band,)),
            dma((n_gy // 2,)), dma((n_gy // 2,)), dma((2 * n_band,)), dma((2 * n_band,)),
            dma((n_gx,)), dma((n_gx,)),
            *[pltpu.SemaphoreType.REGULAR] * 3,
        ],
        compiler_params=pltpu.CompilerParams(
            collective_id=0, has_side_effects=True, vmem_limit_bytes=55008 * 1024
        ),
        cost_estimate=pl.CostEstimate(
            flops=16_000_000, bytes_accessed=4 * 2 * orbitals.size, transcendentals=0
        ),
    )(orbitals, potential)


def solution(mesh):
    sizes = tuple(mesh.shape[axis] for axis in ("gx", "gy", "band"))
    in_specs = (P("band", "gx", "gy", None), P("gx", "gy", None))
    out_specs = P("band", "gx", "gy", None)
    return jax.shard_map(
        functools.partial(local, sizes=sizes),
        mesh=mesh, in_specs=in_specs, out_specs=out_specs, check_vma=False,
    )
```

```python
import functools

import jax
import jax.numpy as jnp
from jax import lax
from jax.experimental import pallas as pl
from jax.experimental.pallas import tpu as pltpu
from jax.sharding import PartitionSpec as P

COEF = (
    -5369.0 / 1800.0,
    12.0 / 7.0,
    -15.0 / 56.0,
    10.0 / 189.0,
    -1.0 / 112.0,
    2.0 / 1925.0,
    -1.0 / 16632.0,
)
LOWER_EDGE = 4.0
UPPER_EDGE = 16.0
BOTTOM_EDGE = -2.5
REACH = 6
MESH = pl.DeviceIdType.MESH


def chebyshev_weights():
    half = (UPPER_EDGE - LOWER_EDGE) / 2.0
    centre = (UPPER_EDGE + LOWER_EDGE) / 2.0
    first = half / (BOTTOM_EDGE - centre)
    rounds = [(first / half, 0.0)]
    now = first
    for _ in range(2):
        following = 1.0 / (2.0 / first - now)
        rounds.append((2.0 * following / half, now * following))
        now = following
    return centre, rounds


CENTRE, ROUNDS = chebyshev_weights()


def split_three(value):
    high = value.astype(jnp.bfloat16)
    rest = value - high.astype(jnp.float32)
    middle = rest.astype(jnp.bfloat16)
    low = (rest - middle.astype(jnp.float32)).astype(jnp.bfloat16)
    return high, middle, low


def kernel(
    sizes, orb_ref, pot_hbm, out_ref, pot_ref, xb, yb, acc, every, fc, sums_gy, sums_band, sums_gx, gram,
    load_sem, x_send, x_recv, y_send, y_recv, a_send, a_recv, ring_send, ring_recv,
    gy_send, gy_recv, band_send, band_recv, gx_send, gx_recv,
    near, middle_way, far,
):
    n_gx, n_gy, n_band = sizes
    n_orb, n_x, n_y, n_z = out_ref.shape
    total = n_orb * n_band
    gx = lax.axis_index("gx")
    gy = lax.axis_index("gy")
    band = lax.axis_index("band")
    me = {"gx": gx, "gy": gy, "band": band}
    counts = {"gx": n_gx, "gy": n_gy, "band": n_band}

    def peer(axis, step):
        return lax.rem(me[axis] + step, counts[axis])

    barrier = pltpu.get_barrier_semaphore()

    def greet(semaphore, axis, distance):
        for step in (distance, counts[axis] - distance):
            pl.semaphore_signal(
                semaphore, inc=1, device_id={axis: peer(axis, step)}, device_id_type=MESH
            )

    for axis in ("gx", "gy", "band"):
        greet(barrier, axis, 1)

    own_x = pl.ds(REACH, n_x)
    own_y = pl.ds(n_y, n_y)
    load_x = pltpu.make_async_copy(orb_ref, xb.at[0, :, own_x], load_sem.at[0])
    load_y = pltpu.make_async_copy(orb_ref, yb.at[0, :, :, own_y], load_sem.at[1])
    load_pot = pltpu.make_async_copy(pot_hbm, pot_ref, load_sem.at[2])
    load_x.start()
    load_y.start()
    load_pot.start()
    load_x.wait()
    load_y.wait()
    pl.semaphore_wait(barrier, 6)

    def halo(r, o):
        right_x = {"gx": peer("gx", 1)}
        left_x = {"gx": peer("gx", n_gx - 1)}
        right_y = {"gy": peer("gy", 1)}
        left_y = {"gy": peer("gy", n_gy - 1)}

        def move(buf, src, dst, send, recv, target):
            return pltpu.make_async_remote_copy(
                src_ref=buf.at[src], dst_ref=buf.at[dst], send_sem=send, recv_sem=recv,
                device_id=target, device_id_type=MESH,
            )

        every = slice(None)
        return (
            move(xb, (r, o, pl.ds(n_x, REACH)), (r, o, pl.ds(0, REACH)),
                 x_send.at[r, 0], x_recv.at[r, 0, o], right_x),
            move(xb, (r, o, pl.ds(REACH, REACH)), (r, o, pl.ds(n_x + REACH, REACH)),
                 x_send.at[r, 1], x_recv.at[r, 1, o], left_x),
            move(yb, (r, o, every, pl.ds(2 * n_y - REACH, REACH)),
                 (r, o, every, pl.ds(n_y - REACH, REACH)),
                 y_send.at[r, 0], y_recv.at[r, 0, o], right_y),
            move(yb, (r, o, every, pl.ds(n_y, REACH)), (r, o, every, pl.ds(2 * n_y, REACH)),
                 y_send.at[r, 1], y_recv.at[r, 1, o], left_y),
        )

    def local_part(r, o):
        scale, back = ROUNDS[r]
        value = xb[r, o, own_x]
        result = scale * ((pot_ref[...] - (1.5 * COEF[0] + CENTRE)) * value)
        if r > 0:
            result = result - back * xb[r - 1, o, own_x]
        flat = value.reshape(n_x * n_y, n_z)
        along_z = jnp.zeros_like(flat)
        for k in range(1, REACH + 1):
            pair = pltpu.roll(flat, k, 1) + pltpu.roll(flat, n_z - k, 1)
            along_z = along_z + (-0.5 * COEF[k] * scale) * pair
        acc[o] = result + along_z.reshape(n_x, n_y, n_z)

    def halo_part(r, o):
        scale = ROUNDS[r][0]
        result = acc[o]
        for k in range(1, REACH + 1):
            pair = xb[r, o, pl.ds(REACH + k, n_x)] + xb[r, o, pl.ds(REACH - k, n_x)]
            pair = pair + yb[r, o, :, pl.ds(n_y + k, n_y)]
            pair = pair + yb[r, o, :, pl.ds(n_y - k, n_y)]
            result = result + (-0.5 * COEF[k] * scale) * pair
        return result

    @pl.loop(0, n_orb)
    def _(o):
        for copy in halo(0, o):
            copy.start()

    greet(near, "band", 1)
    load_pot.wait()

    @pl.loop(0, n_orb)
    def _(o):
        local_part(0, o)

    depth = n_orb * n_y

    def rows_of(index):
        return pl.ds(pl.multiple_of(depth * index, depth), depth)

    def spread(target, o):
        start = pl.multiple_of(o * n_y, n_y)
        return pltpu.make_async_remote_copy(
            src_ref=every.at[band, target, pl.ds(start, n_y)],
            dst_ref=fc.at[pl.ds(pl.multiple_of(depth * band + start, n_y), n_y)],
            send_sem=a_send.at[target], recv_sem=a_recv.at[band],
            device_id={"band": target}, device_id_type=MESH,
        )

    def spread_whole(source, target):
        return pltpu.make_async_remote_copy(
            src_ref=every.at[band, target], dst_ref=fc.at[rows_of(source)],
            send_sem=a_send.at[target], recv_sem=a_recv.at[source],
            device_id={"band": target}, device_id_type=MESH,
        )

    def share(step, where, buf, send, recv):
        return pltpu.make_async_remote_copy(
            src_ref=buf.at[0], dst_ref=buf.at[step], send_sem=send.at[step],
            recv_sem=recv.at[step], device_id=where(step), device_id_type=MESH,
        )

    def by_distance(count):
        return sorted(range(1, count), key=lambda step: min(step, count - step))

    other_core = gy + 1 - 2 * lax.rem(gy, 2)
    band_steps = [0] + by_distance(n_band)
    phases = (
        (
            [2 * step + core for step in band_steps for core in (0, 1) if step + core > 0],
            lambda step: {
                "gy": other_core if step % 2 else gy, "band": peer("band", step // 2)
            },
            sums_band, band_send, band_recv,
        ),
        (
            by_distance(n_gy // 2),
            lambda step: {"gy": peer("gy", 2 * step)},
            sums_gy, gy_send, gy_recv,
        ),
        (
            by_distance(n_gx),
            lambda step: {"gx": peer("gx", step)},
            sums_gx, gx_send, gx_recv,
        ),
    )

    for r in range(3):
        if r == 1:
            pl.semaphore_wait(near, 2)
            greet(middle_way, "band", 2)
        if r == 2:
            pl.semaphore_wait(middle_way, 2)

        @pl.loop(0, n_orb)
        def _(o, r=r):
            for copy in halo(r, o):
                copy.wait_recv()
            result = halo_part(r, o)
            if r < 2:
                xb[r + 1, o, own_x] = result
                yb[r + 1, o, :, own_y] = result
                for copy in halo(r + 1, o):
                    copy.start()
                local_part(r + 1, o)
            else:
                every[band, :, pl.ds(pl.multiple_of(o * n_y, n_y), n_y)] = result
                for step in reversed(by_distance(n_band)):
                    spread(peer("band", step), o).start()

    if n_gx > 8:
        greet(far, "gx", 4)
    fc[rows_of(band)] = every[band, band]
    for step in by_distance(n_band):
        spread_whole(peer("band", step), band).wait_recv()

    parts = []
    for y in range(n_y):
        parts.append(split_three(fc[pl.ds(y, total, stride=n_y), :]))
    stacked = jnp.concatenate([jnp.concatenate(part, axis=0) for part in parts], axis=1)
    blocks = lax.dot_general(
        stacked, stacked, (((1,), (1,)), ((), ())), preferred_element_type=jnp.float32
    )
    blocks = blocks[:total] + blocks[total : 2 * total] + blocks[2 * total :]
    gram[:, : 3 * total] = blocks
    gram[:, 3 * total :] = jnp.zeros((total, n_z - 3 * total), jnp.float32)
    wide = gram[...]
    wide = wide + pltpu.roll(wide, n_z - total, 1) + pltpu.roll(wide, n_z - 2 * total, 1)
    lane = lax.broadcasted_iota(jnp.int32, (8, n_z), 1)
    row = lax.broadcasted_iota(jnp.int32, (8, n_z), 0)
    groups = total // 8
    packed = jnp.where(lane < total, wide[:8], 0.0)
    for q in range(1, groups):
        moved = pltpu.roll(wide[8 * q : 8 * q + 8], total * q, 1)
        packed = jnp.where((lane >= total * q) & (lane < total * (q + 1)), moved, packed)

    def sum_sends(steps, where, value, buf, send, recv):
        buf[0] = value
        for step in reversed(steps):
            share(step, where, buf, send, recv).start()

    def sum_waits(steps, where, value, buf, send, recv):
        for step in steps:
            share(step, where, buf, send, recv).wait_recv()
            value = value + buf[step]
        return value

    half = n_band // 2

    def ring(direction, distance, source):
        width = n_x // 2 if distance == half else n_x
        block = every.at[source, pl.ds(direction * (n_x - width), width)]
        return pltpu.make_async_remote_copy(
            src_ref=block, dst_ref=block, send_sem=ring_send.at[direction, distance - 1],
            recv_sem=ring_recv.at[direction, distance - 1],
            device_id={"band": peer("band", n_band - 1 if direction else 1)},
            device_id_type=MESH,
        )

    def source_at(direction, distance):
        return peer("band", distance if direction else n_band - distance)

    def pass_on(distance):
        for direction in (0, 1):
            source = source_at(direction, distance - 1)
            if distance > 1:
                ring(direction, distance - 1, source).wait_recv()
            ring(direction, distance, source).start()

    first, second, third = phases
    sum_sends(*first[:2], packed, *first[2:])
    pass_on(1)
    packed = sum_waits(*first[:2], packed, *first[2:])
    sum_sends(*second[:2], packed, *second[2:])
    pass_on(2)
    packed = sum_waits(*second[:2], packed, *second[2:])
    if n_gx > 8:
        pl.semaphore_wait(far, 2)
    sum_sends(*third[:2], packed, *third[2:])
    for r in range(3):
        for buf, send in ((xb.at[r, :, pl.ds(0, REACH)], x_send),
                          (yb.at[r, :, :, pl.ds(0, REACH)], y_send)):
            for direction in (0, 1):
                pltpu.make_async_remote_copy(
                    src_ref=buf, dst_ref=buf, send_sem=send.at[r, direction],
                    recv_sem=x_recv.at[0, 0, 0], device_id={"gx": peer("gx", 1)},
                    device_id_type=MESH,
                ).wait_send()
    for step in by_distance(n_band):
        spread_whole(band, peer("band", step)).wait_send()
    for steps, where, buf, send, recv in phases[:2]:
        for step in steps:
            share(step, where, buf, send, recv).wait_send()
    for distance in range(3, half + 1):
        pass_on(distance)
    packed = sum_waits(*third[:2], packed, *third[2:])
    cells_all = float(n_x * n_y * n_z * n_gx * n_gy)
    packed = packed * (1.0 / cells_all)

    tiles = []
    for q in range(groups):
        tile = packed if q == 0 else pltpu.roll(packed, n_z - total * q, 1)
        eye = jnp.where(lax.rem(lane, total) == row + 8 * q, 1.0, 0.0)
        tiles.append(jnp.where(lane < total, tile, eye))
    for home in range(groups):
        columns = [
            [
                jnp.broadcast_to(tiles[q][:, 8 * home + at : 8 * home + at + 1], (8, n_z))
                for q in range(home, groups)
            ]
            for at in range(8)
        ]
        for at in range(8):
            pivot_row = jnp.broadcast_to(tiles[home][at : at + 1, :], (8, n_z))
            reciprocal = 1.0 / jnp.broadcast_to(columns[at][0][at : at + 1, :], (8, n_z))
            factors = [column * reciprocal for column in columns[at]]
            factors[0] = jnp.where(row > at, factors[0], 0.0)
            for factor, q in zip(factors, range(home, groups)):
                tiles[q] = tiles[q] - factor * pivot_row
            for later in range(at + 1, 8):
                value = jnp.broadcast_to(columns[later][0][at : at + 1, :], (8, n_z))
                columns[later] = [
                    column - factor * value for column, factor in zip(columns[later], factors)
                ]
    for q in range(groups):
        diagonal = jnp.sum(jnp.where(lane == row + 8 * q, tiles[q], 0.0), axis=1, keepdims=True)
        tiles[q] = jnp.where(lane < total, 0.0, tiles[q] * lax.rsqrt(diagonal))
    for q in range(groups):
        gram[pl.ds(8 * q, 8), :] = tiles[q]
    mine = gram[pl.ds(pl.multiple_of(8 * (band // 2), 8), 8), :]
    mine = jnp.where(lax.rem(band, 2) == 1, pltpu.roll(mine, 4, 0), mine)
    for direction in (0, 1):
        ring(direction, half, source_at(direction, half)).wait_recv()
    results = [[None] * n_x for _ in range(n_orb)]
    for j in range(total):
        source, o = j // n_orb, j % n_orb
        column = jnp.broadcast_to(mine[:, total + j : total + j + 1], (8, n_z))
        weights = [jnp.broadcast_to(column[i : i + 1, :], (8, n_z)) for i in range(n_orb)]
        for x in range(n_x):
            value = every[source, x, o * n_y : (o + 1) * n_y]
            for i in range(n_orb):
                term = weights[i] * value
                results[i][x] = term if j == 0 else results[i][x] + term
    for i in range(n_orb):
        for x in range(n_x):
            out_ref[i, x] = results[i][x]
    for step in third[0]:
        share(step, *third[1:]).wait_send()
    for direction in (0, 1):
        for distance in range(1, half + 1):
            ring(direction, distance, source_at(direction, distance - 1)).wait_send()


def local(orbitals, potential, sizes):
    n_gx, n_gy, n_band = sizes
    n_orb, n_x, n_y, n_z = orbitals.shape
    total = n_orb * n_band
    f32 = jnp.float32
    dma = pltpu.SemaphoreType.DMA
    vmem = pl.BlockSpec(memory_space=pltpu.VMEM)
    return pl.pallas_call(
        functools.partial(kernel, sizes),
        out_shape=jax.ShapeDtypeStruct(orbitals.shape, f32),
        in_specs=[pl.BlockSpec(memory_space=pl.ANY)] * 2,
        out_specs=vmem,
        scratch_shapes=[
            pltpu.VMEM((n_x, n_y, n_z), f32),
            pltpu.VMEM((3, n_orb, n_x + 2 * REACH, n_y, n_z), f32),
            pltpu.VMEM((3, n_orb, n_x, 3 * n_y, n_z), f32),
            pltpu.VMEM((n_orb, n_x, n_y, n_z), f32),
            pltpu.VMEM((n_band, n_x, n_orb * n_y, n_z), f32),
            pltpu.VMEM((total * n_y, n_z), f32),
            pltpu.VMEM((n_gy // 2, 8, n_z), f32),
            pltpu.VMEM((2 * n_band, 8, n_z), f32),
            pltpu.VMEM((n_gx, 8, n_z), f32),
            pltpu.VMEM((total, n_z), f32),
            dma((3,)),
            dma((3, 2)), dma((3, 2, n_orb)), dma((3, 2)), dma((3, 2, n_orb)),
            dma((n_band,)), dma((n_band,)), dma((2, n_band // 2)), dma((2, n_band // 2)),
            dma((n_gy // 2,)), dma((n_gy // 2,)), dma((2 * n_band,)), dma((2 * n_band,)),
            dma((n_gx,)), dma((n_gx,)),
            *[pltpu.SemaphoreType.REGULAR] * 3,
        ],
        compiler_params=pltpu.CompilerParams(
            collective_id=0, has_side_effects=True, vmem_limit_bytes=55008 * 1024
        ),
        cost_estimate=pl.CostEstimate(
            flops=16_000_000, bytes_accessed=4 * 2 * orbitals.size, transcendentals=0
        ),
    )(orbitals, potential)


def solution(mesh):
    sizes = tuple(mesh.shape[axis] for axis in ("gx", "gy", "band"))
    in_specs = (P("band", "gx", "gy", None), P("gx", "gy", None))
    out_specs = P("band", "gx", "gy", None)
    return jax.shard_map(
        functools.partial(local, sizes=sizes),
        mesh=mesh, in_specs=in_specs, out_specs=out_specs, check_vma=False,
    )
```

```python
import functools

import jax
import jax.numpy as jnp
from jax import lax
from jax.experimental import pallas as pl
from jax.experimental.pallas import tpu as pltpu
from jax.sharding import PartitionSpec as P

COEF = (
    -5369.0 / 1800.0,
    12.0 / 7.0,
    -15.0 / 56.0,
    10.0 / 189.0,
    -1.0 / 112.0,
    2.0 / 1925.0,
    -1.0 / 16632.0,
)
LOWER_EDGE = 4.0
UPPER_EDGE = 16.0
BOTTOM_EDGE = -2.5
REACH = 6
MESH = pl.DeviceIdType.MESH


def chebyshev_weights():
    half = (UPPER_EDGE - LOWER_EDGE) / 2.0
    centre = (UPPER_EDGE + LOWER_EDGE) / 2.0
    first = half / (BOTTOM_EDGE - centre)
    rounds = [(first / half, 0.0)]
    now = first
    for _ in range(2):
        following = 1.0 / (2.0 / first - now)
        rounds.append((2.0 * following / half, now * following))
        now = following
    return centre, rounds


CENTRE, ROUNDS = chebyshev_weights()


def split_three(value):
    high = value.astype(jnp.bfloat16)
    rest = value - high.astype(jnp.float32)
    middle = rest.astype(jnp.bfloat16)
    low = (rest - middle.astype(jnp.float32)).astype(jnp.bfloat16)
    return high, middle, low


def kernel(
    sizes, orb_ref, pot_hbm, out_ref, pot_ref, xb, yb, acc, every, fc, sums_gy, sums_band, sums_gx, gram,
    load_sem, x_send, x_recv, y_send, y_recv, a_send, a_recv, ring_send, ring_recv,
    gy_send, gy_recv, band_send, band_recv, gx_send, gx_recv,
    near, middle_way, far,
):
    n_gx, n_gy, n_band = sizes
    n_orb, n_x, n_y, n_z = out_ref.shape
    total = n_orb * n_band
    gx = lax.axis_index("gx")
    gy = lax.axis_index("gy")
    band = lax.axis_index("band")
    me = {"gx": gx, "gy": gy, "band": band}
    counts = {"gx": n_gx, "gy": n_gy, "band": n_band}

    def peer(axis, step):
        return lax.rem(me[axis] + step, counts[axis])

    barrier = pltpu.get_barrier_semaphore()

    def greet(semaphore, axis, distance):
        for step in (distance, counts[axis] - distance):
            pl.semaphore_signal(
                semaphore, inc=1, device_id={axis: peer(axis, step)}, device_id_type=MESH
            )

    for axis in ("gx", "gy", "band"):
        greet(barrier, axis, 1)

    own_x = pl.ds(REACH, n_x)
    own_y = pl.ds(n_y, n_y)
    load_x = pltpu.make_async_copy(orb_ref, xb.at[0, :, own_x], load_sem.at[0])
    load_y = pltpu.make_async_copy(orb_ref, yb.at[0, :, :, own_y], load_sem.at[1])
    load_pot = pltpu.make_async_copy(pot_hbm, pot_ref, load_sem.at[2])
    load_x.start()
    load_y.start()
    load_pot.start()
    pl.semaphore_wait(barrier, 6)

    def halo(r, o):
        right_x = {"gx": peer("gx", 1)}
        left_x = {"gx": peer("gx", n_gx - 1)}
        right_y = {"gy": peer("gy", 1)}
        left_y = {"gy": peer("gy", n_gy - 1)}

        def move(buf, src, dst, send, recv, target, source=None):
            return pltpu.make_async_remote_copy(
                src_ref=(buf if source is None else source).at[src], dst_ref=buf.at[dst], send_sem=send, recv_sem=recv,
                device_id=target, device_id_type=MESH,
            )

        whole = slice(None)
        if r == 0:
            return (
                move(xb, (o, pl.ds(n_x - REACH, REACH)), (0, o, pl.ds(0, REACH)),
                     x_send.at[0, 0], x_recv.at[0, 0, o], right_x, orb_ref),
                move(xb, (o, pl.ds(0, REACH)), (0, o, pl.ds(n_x + REACH, REACH)),
                     x_send.at[0, 1], x_recv.at[0, 1, o], left_x, orb_ref),
                move(yb, (o,), (0, o, whole, pl.ds(0, n_y)),
                     y_send.at[0, 0], y_recv.at[0, 0, o], right_y, orb_ref),
                move(yb, (o,), (0, o, whole, pl.ds(2 * n_y, n_y)),
                     y_send.at[0, 1], y_recv.at[0, 1, o], left_y, orb_ref),
            )
        return (
            move(xb, (r, o, pl.ds(n_x, REACH)), (r, o, pl.ds(0, REACH)),
                 x_send.at[r, 0], x_recv.at[r, 0, o], right_x),
            move(xb, (r, o, pl.ds(REACH, REACH)), (r, o, pl.ds(n_x + REACH, REACH)),
                 x_send.at[r, 1], x_recv.at[r, 1, o], left_x),
            move(yb, (r, o, whole, pl.ds(2 * n_y - REACH, REACH)),
                 (r, o, whole, pl.ds(n_y - REACH, REACH)),
                 y_send.at[r, 0], y_recv.at[r, 0, o], right_y),
            move(yb, (r, o, whole, pl.ds(n_y, REACH)), (r, o, whole, pl.ds(2 * n_y, REACH)),
                 y_send.at[r, 1], y_recv.at[r, 1, o], left_y),
        )

    def local_part(r, o):
        scale, back = ROUNDS[r]
        value = xb[r, o, own_x]
        result = scale * ((pot_ref[...] - (1.5 * COEF[0] + CENTRE)) * value)
        if r > 0:
            result = result - back * xb[r - 1, o, own_x]
        flat = value.reshape(n_x * n_y, n_z)
        along_z = jnp.zeros_like(flat)
        for k in range(1, REACH + 1):
            pair = pltpu.roll(flat, k, 1) + pltpu.roll(flat, n_z - k, 1)
            along_z = along_z + (-0.5 * COEF[k] * scale) * pair
        acc[o] = result + along_z.reshape(n_x, n_y, n_z)

    def halo_part(r, o):
        scale = ROUNDS[r][0]
        result = acc[o]
        for k in range(1, REACH + 1):
            pair = xb[r, o, pl.ds(REACH + k, n_x)] + xb[r, o, pl.ds(REACH - k, n_x)]
            pair = pair + yb[r, o, :, pl.ds(n_y + k, n_y)]
            pair = pair + yb[r, o, :, pl.ds(n_y - k, n_y)]
            result = result + (-0.5 * COEF[k] * scale) * pair
        return result

    half = n_band // 2

    def ring(direction, distance, source):
        width = n_x // 2 if distance == half else n_x
        block = every.at[source, pl.ds(direction * (n_x - width), width)]
        return pltpu.make_async_remote_copy(
            src_ref=block, dst_ref=block, send_sem=ring_send.at[direction, distance - 1],
            recv_sem=ring_recv.at[direction, distance - 1],
            device_id={"band": peer("band", n_band - 1 if direction else 1)},
            device_id_type=MESH,
        )

    def source_at(direction, distance):
        return peer("band", distance if direction else n_band - distance)

    def pass_on(distance):
        for direction in (0, 1):
            source = source_at(direction, distance - 1)
            if distance > 1:
                ring(direction, distance - 1, source).wait_recv()
            ring(direction, distance, source).start()

    @pl.loop(0, n_orb)
    def _(o):
        for copy in halo(0, o):
            copy.start()

    greet(near, "band", 1)
    load_x.wait()
    load_y.wait()
    load_pot.wait()

    @pl.loop(0, n_orb)
    def _(o):
        local_part(0, o)

    depth = n_orb * n_y

    def rows_of(index):
        return pl.ds(pl.multiple_of(depth * index, depth), depth)

    def spread(target, o):
        start = pl.multiple_of(o * n_y, n_y)
        return pltpu.make_async_remote_copy(
            src_ref=every.at[band, target, pl.ds(start, n_y)],
            dst_ref=fc.at[pl.ds(pl.multiple_of(depth * band + start, n_y), n_y)],
            send_sem=a_send.at[target], recv_sem=a_recv.at[band],
            device_id={"band": target}, device_id_type=MESH,
        )

    def spread_whole(source, target):
        return pltpu.make_async_remote_copy(
            src_ref=every.at[band, target], dst_ref=fc.at[rows_of(source)],
            send_sem=a_send.at[target], recv_sem=a_recv.at[source],
            device_id={"band": target}, device_id_type=MESH,
        )

    def share(step, where, buf, send, recv):
        return pltpu.make_async_remote_copy(
            src_ref=buf.at[0], dst_ref=buf.at[step], send_sem=send.at[step],
            recv_sem=recv.at[step], device_id=where(step), device_id_type=MESH,
        )

    def by_distance(count):
        return sorted(range(1, count), key=lambda step: min(step, count - step))

    other_core = gy + 1 - 2 * lax.rem(gy, 2)
    band_steps = [0] + by_distance(n_band)
    phases = (
        (
            [2 * step + core for step in band_steps for core in (0, 1) if step + core > 0],
            lambda step: {
                "gy": other_core if step % 2 else gy, "band": peer("band", step // 2)
            },
            sums_band, band_send, band_recv,
        ),
        (
            by_distance(n_gy // 2),
            lambda step: {"gy": peer("gy", 2 * step)},
            sums_gy, gy_send, gy_recv,
        ),
        (
            by_distance(n_gx),
            lambda step: {"gx": peer("gx", step)},
            sums_gx, gx_send, gx_recv,
        ),
    )

    for r in range(3):
        if r == 1:
            pl.semaphore_wait(near, 2)
            greet(middle_way, "band", 2)
        if r == 2:
            pl.semaphore_wait(middle_way, 2)

        @pl.loop(0, n_orb)
        def _(o, r=r):
            for copy in halo(r, o):
                copy.wait_recv()
            result = halo_part(r, o)
            if r < 2:
                xb[r + 1, o, own_x] = result
                yb[r + 1, o, :, own_y] = result
                for copy in halo(r + 1, o):
                    copy.start()
            else:
                every[band, :, pl.ds(pl.multiple_of(o * n_y, n_y), n_y)] = result
                for step in reversed(by_distance(n_band)):
                    spread(peer("band", step), o).start()

        if r < 2:
            @pl.loop(0, n_orb)
            def _(o, r=r):
                local_part(r + 1, o)

    pass_on(1)
    if n_gx > 8:
        greet(far, "gx", 4)
    fc[rows_of(band)] = every[band, band]
    for step in by_distance(n_band):
        spread_whole(peer("band", step), band).wait_recv()

    parts = []
    for y in range(n_y):
        parts.append(split_three(fc[pl.ds(y, total, stride=n_y), :]))
    stacked = jnp.concatenate([jnp.concatenate(part, axis=0) for part in parts], axis=1)
    blocks = lax.dot_general(
        stacked, stacked, (((1,), (1,)), ((), ())), preferred_element_type=jnp.float32
    )
    blocks = blocks[:total] + blocks[total : 2 * total] + blocks[2 * total :]
    gram[:, : 3 * total] = blocks
    gram[:, 3 * total :] = jnp.zeros((total, n_z - 3 * total), jnp.float32)
    wide = gram[...]
    wide = wide + pltpu.roll(wide, n_z - total, 1) + pltpu.roll(wide, n_z - 2 * total, 1)
    lane = lax.broadcasted_iota(jnp.int32, (8, n_z), 1)
    row = lax.broadcasted_iota(jnp.int32, (8, n_z), 0)
    groups = total // 8
    packed = jnp.where(lane < total, wide[:8], 0.0)
    for q in range(1, groups):
        moved = pltpu.roll(wide[8 * q : 8 * q + 8], total * q, 1)
        packed = jnp.where((lane >= total * q) & (lane < total * (q + 1)), moved, packed)

    def sum_sends(steps, where, value, buf, send, recv):
        buf[0] = value
        for step in reversed(steps):
            share(step, where, buf, send, recv).start()

    def sum_waits(steps, where, value, buf, send, recv):
        for step in steps:
            share(step, where, buf, send, recv).wait_recv()
            value = value + buf[step]
        return value

    first, second, third = phases
    sum_sends(*first[:2], packed, *first[2:])
    pass_on(2)
    packed = sum_waits(*first[:2], packed, *first[2:])
    sum_sends(*second[:2], packed, *second[2:])
    pass_on(3)
    packed = sum_waits(*second[:2], packed, *second[2:])
    if n_gx > 8:
        pl.semaphore_wait(far, 2)
    sum_sends(*third[:2], packed, *third[2:])
    for r in range(3):
        for buf, send in ((xb.at[r, :, pl.ds(0, REACH)], x_send),
                          (yb.at[r, :, :, pl.ds(0, REACH if r else n_y)], y_send)):
            for direction in (0, 1):
                pltpu.make_async_remote_copy(
                    src_ref=buf, dst_ref=buf, send_sem=send.at[r, direction],
                    recv_sem=x_recv.at[0, 0, 0], device_id={"gx": peer("gx", 1)},
                    device_id_type=MESH,
                ).wait_send()
    for step in by_distance(n_band):
        spread_whole(band, peer("band", step)).wait_send()
    for steps, where, buf, send, recv in phases[:2]:
        for step in steps:
            share(step, where, buf, send, recv).wait_send()
    for distance in range(4, half + 1):
        pass_on(distance)
    packed = sum_waits(*third[:2], packed, *third[2:])
    cells_all = float(n_x * n_y * n_z * n_gx * n_gy)
    packed = packed * (1.0 / cells_all)

    tiles = []
    for q in range(groups):
        tile = packed if q == 0 else pltpu.roll(packed, n_z - total * q, 1)
        eye = jnp.where(lax.rem(lane, total) == row + 8 * q, 1.0, 0.0)
        tiles.append(jnp.where(lane < total, tile, eye))
    for home in range(groups):
        columns = [
            [
                jnp.broadcast_to(tiles[q][:, 8 * home + at : 8 * home + at + 1], (8, n_z))
                for q in range(home, groups)
            ]
            for at in range(8)
        ]
        for at in range(8):
            pivot_row = jnp.broadcast_to(tiles[home][at : at + 1, :], (8, n_z))
            reciprocal = 1.0 / jnp.broadcast_to(columns[at][0][at : at + 1, :], (8, n_z))
            factors = [column * reciprocal for column in columns[at]]
            factors[0] = jnp.where(row > at, factors[0], 0.0)
            for factor, q in zip(factors, range(home, groups)):
                tiles[q] = tiles[q] - factor * pivot_row
            for later in range(at + 1, 8):
                value = jnp.broadcast_to(columns[later][0][at : at + 1, :], (8, n_z))
                columns[later] = [
                    column - factor * value for column, factor in zip(columns[later], factors)
                ]
    for q in range(groups):
        diagonal = jnp.sum(jnp.where(lane == row + 8 * q, tiles[q], 0.0), axis=1, keepdims=True)
        tiles[q] = jnp.where(lane < total, 0.0, tiles[q] * lax.rsqrt(diagonal))
    for q in range(groups):
        gram[pl.ds(8 * q, 8), :] = tiles[q]
    mine = gram[pl.ds(pl.multiple_of(8 * (band // 2), 8), 8), :]
    mine = jnp.where(lax.rem(band, 2) == 1, pltpu.roll(mine, 4, 0), mine)
    for direction in (0, 1):
        ring(direction, half, source_at(direction, half)).wait_recv()
    results = [[None] * n_x for _ in range(n_orb)]
    for j in range(total):
        source, o = j // n_orb, j % n_orb
        column = jnp.broadcast_to(mine[:, total + j : total + j + 1], (8, n_z))
        weights = [jnp.broadcast_to(column[i : i + 1, :], (8, n_z)) for i in range(n_orb)]
        for x in range(n_x):
            value = every[source, x, o * n_y : (o + 1) * n_y]
            for i in range(n_orb):
                term = weights[i] * value
                results[i][x] = term if j == 0 else results[i][x] + term
    for i in range(n_orb):
        for x in range(n_x):
            out_ref[i, x] = results[i][x]
    for step in third[0]:
        share(step, *third[1:]).wait_send()
    for direction in (0, 1):
        for distance in range(1, half + 1):
            ring(direction, distance, source_at(direction, distance - 1)).wait_send()


def local(orbitals, potential, sizes):
    n_gx, n_gy, n_band = sizes
    n_orb, n_x, n_y, n_z = orbitals.shape
    total = n_orb * n_band
    f32 = jnp.float32
    dma = pltpu.SemaphoreType.DMA
    vmem = pl.BlockSpec(memory_space=pltpu.VMEM)
    return pl.pallas_call(
        functools.partial(kernel, sizes),
        out_shape=jax.ShapeDtypeStruct(orbitals.shape, f32),
        in_specs=[pl.BlockSpec(memory_space=pl.ANY)] * 2,
        out_specs=vmem,
        scratch_shapes=[
            pltpu.VMEM((n_x, n_y, n_z), f32),
            pltpu.VMEM((3, n_orb, n_x + 2 * REACH, n_y, n_z), f32),
            pltpu.VMEM((3, n_orb, n_x, 3 * n_y, n_z), f32),
            pltpu.VMEM((n_orb, n_x, n_y, n_z), f32),
            pltpu.VMEM((n_band, n_x, n_orb * n_y, n_z), f32),
            pltpu.VMEM((total * n_y, n_z), f32),
            pltpu.VMEM((n_gy // 2, 8, n_z), f32),
            pltpu.VMEM((2 * n_band, 8, n_z), f32),
            pltpu.VMEM((n_gx, 8, n_z), f32),
            pltpu.VMEM((total, n_z), f32),
            dma((3,)),
            dma((3, 2)), dma((3, 2, n_orb)), dma((3, 2)), dma((3, 2, n_orb)),
            dma((n_band,)), dma((n_band,)), dma((2, n_band // 2)), dma((2, n_band // 2)),
            dma((n_gy // 2,)), dma((n_gy // 2,)), dma((2 * n_band,)), dma((2 * n_band,)),
            dma((n_gx,)), dma((n_gx,)),
            *[pltpu.SemaphoreType.REGULAR] * 3,
        ],
        compiler_params=pltpu.CompilerParams(
            collective_id=0, has_side_effects=True, vmem_limit_bytes=32 * 1024 * 1024
        ),
        cost_estimate=pl.CostEstimate(
            flops=16_000_000, bytes_accessed=4 * 2 * orbitals.size, transcendentals=0
        ),
    )(
        pltpu.with_memory_space_constraint(orbitals, pltpu.HBM),
        pltpu.with_memory_space_constraint(potential, pltpu.HBM),
    )


def solution(mesh):
    sizes = tuple(mesh.shape[axis] for axis in ("gx", "gy", "band"))
    in_specs = (P("band", "gx", "gy", None), P("gx", "gy", None))
    out_specs = P("band", "gx", "gy", None)
    return jax.shard_map(
        functools.partial(local, sizes=sizes),
        mesh=mesh, in_specs=in_specs, out_specs=out_specs, check_vma=False,
    )
```

```python
import functools

import jax
import jax.numpy as jnp
from jax import lax
from jax.experimental import pallas as pl
from jax.experimental.pallas import tpu as pltpu
from jax.sharding import PartitionSpec as P

COEF = (
    -5369.0 / 1800.0,
    12.0 / 7.0,
    -15.0 / 56.0,
    10.0 / 189.0,
    -1.0 / 112.0,
    2.0 / 1925.0,
    -1.0 / 16632.0,
)
LOWER_EDGE = 4.0
UPPER_EDGE = 16.0
BOTTOM_EDGE = -2.5
REACH = 6
MESH = pl.DeviceIdType.MESH


def chebyshev_weights():
    half = (UPPER_EDGE - LOWER_EDGE) / 2.0
    centre = (UPPER_EDGE + LOWER_EDGE) / 2.0
    first = half / (BOTTOM_EDGE - centre)
    rounds = [(first / half, 0.0)]
    now = first
    for _ in range(2):
        following = 1.0 / (2.0 / first - now)
        rounds.append((2.0 * following / half, now * following))
        now = following
    return centre, rounds


CENTRE, ROUNDS = chebyshev_weights()


def split_two(value):
    high = value.astype(jnp.bfloat16)
    return high, (value - high.astype(jnp.float32)).astype(jnp.bfloat16)


def kernel(
    sizes, orb_ref, pot_hbm, out_ref, pot_ref, xb, yb, acc, every, fc, sums_gy, sums_band, sums_gx, gram,
    load_sem, x_send, x_recv, y_send, y_recv, a_send, a_recv, ring_send, ring_recv,
    gy_send, gy_recv, band_send, band_recv, gx_send, gx_recv,
    near, middle_way, far,
):
    n_gx, n_gy, n_band = sizes
    n_orb, n_x, n_y, n_z = out_ref.shape
    total = n_orb * n_band
    gx = lax.axis_index("gx")
    gy = lax.axis_index("gy")
    band = lax.axis_index("band")
    me = {"gx": gx, "gy": gy, "band": band}
    counts = {"gx": n_gx, "gy": n_gy, "band": n_band}

    ring_of = {
        axis: [lax.rem(me[axis] + step, counts[axis]) for step in range(counts[axis])]
        for axis in ("gx", "gy", "band")
    }

    def peer(axis, step):
        return ring_of[axis][step % counts[axis]]

    def device(**where):
        return tuple(where.get(axis, me[axis]) for axis in ("gx", "gy", "band"))

    barrier = pltpu.get_barrier_semaphore()

    def greet(semaphore, axis, distance):
        for step in (distance, counts[axis] - distance):
            pl.semaphore_signal(
                semaphore, inc=1, device_id=device(**{axis: peer(axis, step)}), device_id_type=MESH
            )

    for axis in ("gx", "gy", "band"):
        greet(barrier, axis, 1)

    own_x = pl.ds(REACH, n_x)
    own_y = pl.ds(n_y, n_y)
    load_x = pltpu.make_async_copy(orb_ref, xb.at[0, :, own_x], load_sem.at[0])
    load_y = pltpu.make_async_copy(orb_ref, yb.at[0, :, :, own_y], load_sem.at[1])
    load_pot = pltpu.make_async_copy(pot_hbm, pot_ref, load_sem.at[2])
    load_x.start()
    load_y.start()
    load_pot.start()
    pl.semaphore_wait(barrier, 6)

    def halo(r, o):
        right_x = {"gx": peer("gx", 1)}
        left_x = {"gx": peer("gx", n_gx - 1)}
        right_y = {"gy": peer("gy", 1)}
        left_y = {"gy": peer("gy", n_gy - 1)}

        def move(buf, src, dst, send, recv, target, source=None):
            return pltpu.make_async_remote_copy(
                src_ref=(buf if source is None else source).at[src], dst_ref=buf.at[dst], send_sem=send, recv_sem=recv,
                device_id=device(**target), device_id_type=MESH,
            )

        whole = slice(None)
        if r == 0:
            return (
                move(xb, (o, pl.ds(n_x - REACH, REACH)), (0, o, pl.ds(0, REACH)),
                     x_send.at[0, 0], x_recv.at[0, 0, o], right_x, orb_ref),
                move(xb, (o, pl.ds(0, REACH)), (0, o, pl.ds(n_x + REACH, REACH)),
                     x_send.at[0, 1], x_recv.at[0, 1, o], left_x, orb_ref),
                move(yb, (o,), (0, o, whole, pl.ds(0, n_y)),
                     y_send.at[0, 0], y_recv.at[0, 0, o], right_y, orb_ref),
                move(yb, (o,), (0, o, whole, pl.ds(2 * n_y, n_y)),
                     y_send.at[0, 1], y_recv.at[0, 1, o], left_y, orb_ref),
            )
        return (
            move(xb, (r, o, pl.ds(n_x, REACH)), (r, o, pl.ds(0, REACH)),
                 x_send.at[r, 0], x_recv.at[r, 0, o], right_x),
            move(xb, (r, o, pl.ds(REACH, REACH)), (r, o, pl.ds(n_x + REACH, REACH)),
                 x_send.at[r, 1], x_recv.at[r, 1, o], left_x),
            move(yb, (r, o, whole, pl.ds(2 * n_y - REACH, REACH)),
                 (r, o, whole, pl.ds(n_y - REACH, REACH)),
                 y_send.at[r, 0], y_recv.at[r, 0, o], right_y),
            move(yb, (r, o, whole, pl.ds(n_y, REACH)), (r, o, whole, pl.ds(2 * n_y, REACH)),
                 y_send.at[r, 1], y_recv.at[r, 1, o], left_y),
        )

    def local_part(r, o):
        scale, back = ROUNDS[r]
        value = xb[r, o, own_x]
        result = scale * ((pot_ref[...] - (1.5 * COEF[0] + CENTRE)) * value)
        if r > 0:
            result = result - back * xb[r - 1, o, own_x]
        flat = value.reshape(n_x * n_y, n_z)
        along_z = jnp.zeros_like(flat)
        for k in range(1, REACH + 1):
            pair = pltpu.roll(flat, k, 1) + pltpu.roll(flat, n_z - k, 1)
            along_z = along_z + (-0.5 * COEF[k] * scale) * pair
        acc[o] = result + along_z.reshape(n_x, n_y, n_z)

    def halo_part(r, o):
        scale = ROUNDS[r][0]
        result = acc[o]
        for k in range(1, REACH + 1):
            pair = xb[r, o, pl.ds(REACH + k, n_x)] + xb[r, o, pl.ds(REACH - k, n_x)]
            pair = pair + yb[r, o, :, pl.ds(n_y + k, n_y)]
            pair = pair + yb[r, o, :, pl.ds(n_y - k, n_y)]
            result = result + (-0.5 * COEF[k] * scale) * pair
        return result

    half = n_band // 2

    def ring(direction, distance, source):
        width = n_x // 2 if distance == half else n_x
        block = every.at[source, pl.ds(direction * (n_x - width), width)]
        return pltpu.make_async_remote_copy(
            src_ref=block, dst_ref=block, send_sem=ring_send.at[direction, distance - 1],
            recv_sem=ring_recv.at[direction, distance - 1],
            device_id=device(band=peer("band", n_band - 1 if direction else 1)),
            device_id_type=MESH,
        )

    def source_at(direction, distance):
        return peer("band", distance if direction else n_band - distance)

    def pass_on(distance):
        for direction in (0, 1):
            source = source_at(direction, distance - 1)
            if distance > 1:
                ring(direction, distance - 1, source).wait_recv()
            ring(direction, distance, source).start()

    @pl.loop(0, n_orb)
    def _(o):
        for copy in halo(0, o):
            copy.start()

    greet(near, "band", 1)
    load_x.wait()
    load_y.wait()
    load_pot.wait()

    @pl.loop(0, n_orb)
    def _(o):
        local_part(0, o)

    depth = n_orb * n_y

    def rows_of(index):
        return pl.ds(pl.multiple_of(depth * index, depth), depth)

    def spread(target, o):
        start = pl.multiple_of(o * n_y, n_y)
        return pltpu.make_async_remote_copy(
            src_ref=every.at[band, target, pl.ds(start, n_y)],
            dst_ref=fc.at[pl.ds(pl.multiple_of(depth * band + start, n_y), n_y)],
            send_sem=a_send.at[target], recv_sem=a_recv.at[band],
            device_id=device(band=target), device_id_type=MESH,
        )

    def spread_whole(source, target):
        return pltpu.make_async_remote_copy(
            src_ref=every.at[band, target], dst_ref=fc.at[rows_of(source)],
            send_sem=a_send.at[target], recv_sem=a_recv.at[source],
            device_id=device(band=target), device_id_type=MESH,
        )

    def share(step, where, buf, send, recv):
        return pltpu.make_async_remote_copy(
            src_ref=buf.at[0], dst_ref=buf.at[step], send_sem=send.at[0],
            recv_sem=recv.at[step], device_id=device(**where(step)), device_id_type=MESH,
        )

    def sum_sent(steps, where, buf, send, recv):
        if steps:
            sent = buf.at[pl.ds(1, len(steps))]
            pltpu.make_async_remote_copy(
                src_ref=sent, dst_ref=sent, send_sem=send.at[0], recv_sem=recv.at[1],
                device_id=device(**where(steps[0])), device_id_type=MESH,
            ).wait_send()

    def by_distance(count):
        return sorted(range(1, count), key=lambda step: min(step, count - step))

    other_core = gy + 1 - 2 * lax.rem(gy, 2)
    band_steps = [0] + by_distance(n_band)
    phases = (
        (
            [2 * step + core for step in band_steps for core in (0, 1) if step + core > 0],
            lambda step: {
                "gy": other_core if step % 2 else gy, "band": peer("band", step // 2)
            },
            sums_band, band_send, band_recv,
        ),
        (
            by_distance(n_gy // 2),
            lambda step: {"gy": peer("gy", 2 * step)},
            sums_gy, gy_send, gy_recv,
        ),
        (
            by_distance(n_gx),
            lambda step: {"gx": peer("gx", step)},
            sums_gx, gx_send, gx_recv,
        ),
    )

    for r in range(3):
        if r == 1:
            pl.semaphore_wait(near, 2)
            greet(middle_way, "band", 2)
        if r == 2:
            pl.semaphore_wait(middle_way, 2)

        @pl.loop(0, n_orb)
        def _(o, r=r):
            for copy in halo(r, o):
                copy.wait_recv()
            result = halo_part(r, o)
            if r < 2:
                xb[r + 1, o, own_x] = result
                yb[r + 1, o, :, own_y] = result
                for copy in halo(r + 1, o):
                    copy.start()
            else:
                every[band, :, pl.ds(pl.multiple_of(o * n_y, n_y), n_y)] = result
                for step in reversed(by_distance(n_band)):
                    spread(peer("band", step), o).start()

        if r < 2:
            @pl.loop(0, n_orb)
            def _(o, r=r):
                local_part(r + 1, o)

    pass_on(1)
    if n_gx > 8:
        greet(far, "gx", 4)
    fc[rows_of(band)] = every[band, band]
    for step in by_distance(n_band):
        spread_whole(peer("band", step), band).wait_recv()

    parts = []
    for y in range(n_y):
        parts.append(split_two(fc[pl.ds(y, total, stride=n_y), :]))
    stacked = jnp.concatenate([jnp.concatenate(part, axis=0) for part in parts], axis=1)
    blocks = lax.dot_general(
        stacked, stacked, (((1,), (1,)), ((), ())), preferred_element_type=jnp.float32
    )
    blocks = blocks[:total] + blocks[total:]
    gram[:, : 2 * total] = blocks
    gram[:, 2 * total :] = jnp.zeros((total, n_z - 2 * total), jnp.float32)
    wide = gram[...]
    wide = wide + pltpu.roll(wide, n_z - total, 1)
    lane = lax.broadcasted_iota(jnp.int32, (8, n_z), 1)
    row = lax.broadcasted_iota(jnp.int32, (8, n_z), 0)
    groups = total // 8
    packed = jnp.where(lane < total, wide[:8], 0.0)
    for q in range(1, groups):
        moved = pltpu.roll(wide[8 * q : 8 * q + 8], total * q, 1)
        packed = jnp.where((lane >= total * q) & (lane < total * (q + 1)), moved, packed)

    def sum_sends(steps, where, value, buf, send, recv):
        buf[0] = value
        for step in reversed(steps):
            share(step, where, buf, send, recv).start()

    def sum_waits(steps, where, value, buf, send, recv):
        for step in steps:
            share(step, where, buf, send, recv).wait_recv()
            value = value + buf[step]
        return value

    first, second, third = phases
    sum_sends(*first[:2], packed, *first[2:])
    pass_on(2)
    packed = sum_waits(*first[:2], packed, *first[2:])
    sum_sends(*second[:2], packed, *second[2:])
    pass_on(3)
    packed = sum_waits(*second[:2], packed, *second[2:])
    if n_gx > 8:
        pl.semaphore_wait(far, 2)
    sum_sends(*third[:2], packed, *third[2:])
    for r in range(3):
        for buf, send in ((xb.at[r, :, pl.ds(0, REACH)], x_send),
                          (yb.at[r, :, :, pl.ds(0, REACH if r else n_y)], y_send)):
            for direction in (0, 1):
                pltpu.make_async_remote_copy(
                    src_ref=buf, dst_ref=buf, send_sem=send.at[r, direction],
                    recv_sem=x_recv.at[0, 0, 0], device_id=device(gx=peer("gx", 1)),
                    device_id_type=MESH,
                ).wait_send()
    for step in by_distance(n_band):
        spread_whole(band, peer("band", step)).wait_send()
    sum_sent(*first)
    sum_sent(*second)
    for distance in range(4, half + 1):
        pass_on(distance)
    for direction in (0, 1):
        for distance in (1, 2):
            ring(direction, distance, source_at(direction, distance - 1)).wait_send()
    packed = sum_waits(*third[:2], packed, *third[2:])
    cells_all = float(n_x * n_y * n_z * n_gx * n_gy)
    packed = packed * (1.0 / cells_all)

    tiles = []
    for q in range(groups):
        tile = packed if q == 0 else pltpu.roll(packed, n_z - total * q, 1)
        eye = jnp.where(lax.rem(lane, total) == row + 8 * q, 1.0, 0.0)
        tiles.append(jnp.where(lane < total, tile, eye))
    for home in range(groups):
        columns = [
            [
                jnp.broadcast_to(tiles[q][:, 8 * home + at : 8 * home + at + 1], (8, n_z))
                for q in range(home, groups)
            ]
            for at in range(8)
        ]
        for at in range(8):
            pivot_row = jnp.broadcast_to(tiles[home][at : at + 1, :], (8, n_z))
            reciprocal = 1.0 / jnp.broadcast_to(columns[at][0][at : at + 1, :], (8, n_z))
            factors = [column * reciprocal for column in columns[at]]
            factors[0] = jnp.where(row > at, factors[0], 0.0)
            for factor, q in zip(factors, range(home, groups)):
                tiles[q] = tiles[q] - factor * pivot_row
            for later in range(at + 1, 8):
                value = jnp.broadcast_to(columns[later][0][at : at + 1, :], (8, n_z))
                columns[later] = [
                    column - factor * value for column, factor in zip(columns[later], factors)
                ]
    for q in range(groups):
        diagonal = jnp.sum(jnp.where(lane == row + 8 * q, tiles[q], 0.0), axis=1, keepdims=True)
        tiles[q] = jnp.where(lane < total, 0.0, tiles[q] * lax.rsqrt(diagonal))
    for q in range(groups):
        gram[pl.ds(8 * q, 8), :] = tiles[q]
    mine = gram[pl.ds(pl.multiple_of(8 * (band // 2), 8), 8), :]
    mine = jnp.where(lax.rem(band, 2) == 1, pltpu.roll(mine, 4, 0), mine)
    for direction in (0, 1):
        ring(direction, half, source_at(direction, half)).wait_recv()
    results = [[None] * n_x for _ in range(n_orb)]
    for j in range(total):
        source, o = j // n_orb, j % n_orb
        column = jnp.broadcast_to(mine[:, total + j : total + j + 1], (8, n_z))
        weights = [jnp.broadcast_to(column[i : i + 1, :], (8, n_z)) for i in range(n_orb)]
        for x in range(n_x):
            value = every[source, x, o * n_y : (o + 1) * n_y]
            for i in range(n_orb):
                term = weights[i] * value
                results[i][x] = term if j == 0 else results[i][x] + term
    for i in range(n_orb):
        for x in range(n_x):
            out_ref[i, x] = results[i][x]
    sum_sent(*third)
    for direction in (0, 1):
        for distance in range(3, half + 1):
            ring(direction, distance, source_at(direction, distance - 1)).wait_send()


def local(orbitals, potential, sizes):
    n_gx, n_gy, n_band = sizes
    n_orb, n_x, n_y, n_z = orbitals.shape
    total = n_orb * n_band
    f32 = jnp.float32
    dma = pltpu.SemaphoreType.DMA
    vmem = pl.BlockSpec(memory_space=pltpu.VMEM)
    return pl.pallas_call(
        functools.partial(kernel, sizes),
        out_shape=jax.ShapeDtypeStruct(orbitals.shape, f32),
        in_specs=[pl.BlockSpec(memory_space=pl.ANY)] * 2,
        out_specs=vmem,
        scratch_shapes=[
            pltpu.VMEM((n_x, n_y, n_z), f32),
            pltpu.VMEM((3, n_orb, n_x + 2 * REACH, n_y, n_z), f32),
            pltpu.VMEM((3, n_orb, n_x, 3 * n_y, n_z), f32),
            pltpu.VMEM((n_orb, n_x, n_y, n_z), f32),
            pltpu.VMEM((n_band, n_x, n_orb * n_y, n_z), f32),
            pltpu.VMEM((total * n_y, n_z), f32),
            pltpu.VMEM((n_gy // 2, 8, n_z), f32),
            pltpu.VMEM((2 * n_band, 8, n_z), f32),
            pltpu.VMEM((n_gx, 8, n_z), f32),
            pltpu.VMEM((total, n_z), f32),
            dma((3,)),
            dma((3, 2)), dma((3, 2, n_orb)), dma((3, 2)), dma((3, 2, n_orb)),
            dma((n_band,)), dma((n_band,)), dma((2, n_band // 2)), dma((2, n_band // 2)),
            dma((n_gy // 2,)), dma((n_gy // 2,)), dma((2 * n_band,)), dma((2 * n_band,)),
            dma((n_gx,)), dma((n_gx,)),
            *[pltpu.SemaphoreType.REGULAR] * 3,
        ],
        compiler_params=pltpu.CompilerParams(
            collective_id=0, has_side_effects=True, vmem_limit_bytes=32 * 1024 * 1024
        ),
        cost_estimate=pl.CostEstimate(
            flops=16_000_000, bytes_accessed=4 * 2 * orbitals.size, transcendentals=0
        ),
    )(
        pltpu.with_memory_space_constraint(orbitals, pltpu.HBM),
        pltpu.with_memory_space_constraint(potential, pltpu.HBM),
    )


def solution(mesh):
    sizes = tuple(mesh.shape[axis] for axis in ("gx", "gy", "band"))
    in_specs = (P("band", "gx", "gy", None), P("gx", "gy", None))
    out_specs = P("band", "gx", "gy", None)
    return jax.shard_map(
        functools.partial(local, sizes=sizes),
        mesh=mesh, in_specs=in_specs, out_specs=out_specs, check_vma=False,
    )
```

```python
import functools

import jax
import jax.numpy as jnp
from jax import lax
from jax.experimental import pallas as pl
from jax.experimental.pallas import tpu as pltpu
from jax.sharding import PartitionSpec as P

COEF = (
    -5369.0 / 1800.0,
    12.0 / 7.0,
    -15.0 / 56.0,
    10.0 / 189.0,
    -1.0 / 112.0,
    2.0 / 1925.0,
    -1.0 / 16632.0,
)
LOWER_EDGE = 4.0
UPPER_EDGE = 16.0
BOTTOM_EDGE = -2.5
REACH = 6
MESH = pl.DeviceIdType.MESH


def chebyshev_weights():
    half = (UPPER_EDGE - LOWER_EDGE) / 2.0
    centre = (UPPER_EDGE + LOWER_EDGE) / 2.0
    first = half / (BOTTOM_EDGE - centre)
    rounds = [(first / half, 0.0)]
    now = first
    for _ in range(2):
        following = 1.0 / (2.0 / first - now)
        rounds.append((2.0 * following / half, now * following))
        now = following
    return centre, rounds


CENTRE, ROUNDS = chebyshev_weights()


def split_two(value):
    high = value.astype(jnp.bfloat16)
    return high, (value - high.astype(jnp.float32)).astype(jnp.bfloat16)


def kernel(
    sizes, orb_ref, pot_hbm, out_ref, pot_ref, xb, yb, acc, every, fc, sums_gy, sums_band, sums_gx, gram,
    load_sem, x_send, x_recv, y_send, y_recv, a_send, a_recv, ring_send, ring_recv,
    gy_send, gy_recv, band_send, band_recv, gx_send, gx_recv,
    near, middle_way, far,
):
    n_gx, n_gy, n_band = sizes
    n_orb, n_x, n_y, n_z = out_ref.shape
    total = n_orb * n_band
    gx = lax.axis_index("gx")
    gy = lax.axis_index("gy")
    band = lax.axis_index("band")
    me = {"gx": gx, "gy": gy, "band": band}
    counts = {"gx": n_gx, "gy": n_gy, "band": n_band}

    ring_of = {
        axis: [lax.rem(me[axis] + step, counts[axis]) for step in range(counts[axis])]
        for axis in ("gx", "gy", "band")
    }

    def peer(axis, step):
        return ring_of[axis][step % counts[axis]]

    def device(**where):
        return tuple(where.get(axis, me[axis]) for axis in ("gx", "gy", "band"))

    barrier = pltpu.get_barrier_semaphore()

    def greet(semaphore, axis, distance):
        for step in (distance, counts[axis] - distance):
            pl.semaphore_signal(
                semaphore, inc=1, device_id=device(**{axis: peer(axis, step)}), device_id_type=MESH
            )

    for axis in ("gx", "gy", "band"):
        greet(barrier, axis, 1)

    own_x = pl.ds(REACH, n_x)
    own_y = pl.ds(n_y, n_y)
    load_x = pltpu.make_async_copy(orb_ref, xb.at[0, :, own_x], load_sem.at[0])
    load_y = pltpu.make_async_copy(orb_ref, yb.at[0, :, :, own_y], load_sem.at[1])
    load_pot = pltpu.make_async_copy(pot_hbm, pot_ref, load_sem.at[2])
    load_x.start()
    load_y.start()
    load_pot.start()
    pl.semaphore_wait(barrier, 6)

    def halo(r, o):
        right_x = {"gx": peer("gx", 1)}
        left_x = {"gx": peer("gx", n_gx - 1)}
        right_y = {"gy": peer("gy", 1)}
        left_y = {"gy": peer("gy", n_gy - 1)}

        def move(buf, src, dst, send, recv, target, source=None):
            return pltpu.make_async_remote_copy(
                src_ref=(buf if source is None else source).at[src], dst_ref=buf.at[dst], send_sem=send, recv_sem=recv,
                device_id=device(**target), device_id_type=MESH,
            )

        whole = slice(None)
        if r == 0:
            return (
                move(xb, (o, pl.ds(n_x - REACH, REACH)), (0, o, pl.ds(0, REACH)),
                     x_send.at[0, 0], x_recv.at[0, 0, o], right_x, orb_ref),
                move(xb, (o, pl.ds(0, REACH)), (0, o, pl.ds(n_x + REACH, REACH)),
                     x_send.at[0, 1], x_recv.at[0, 1, o], left_x, orb_ref),
                move(yb, (o,), (0, o, whole, pl.ds(0, n_y)),
                     y_send.at[0, 0], y_recv.at[0, 0, o], right_y, orb_ref),
                move(yb, (o,), (0, o, whole, pl.ds(2 * n_y, n_y)),
                     y_send.at[0, 1], y_recv.at[0, 1, o], left_y, orb_ref),
            )
        return (
            move(xb, (r, o, pl.ds(n_x, REACH)), (r, o, pl.ds(0, REACH)),
                 x_send.at[r, 0], x_recv.at[r, 0, o], right_x),
            move(xb, (r, o, pl.ds(REACH, REACH)), (r, o, pl.ds(n_x + REACH, REACH)),
                 x_send.at[r, 1], x_recv.at[r, 1, o], left_x),
            move(yb, (r, o, whole, pl.ds(2 * n_y - REACH, REACH)),
                 (r, o, whole, pl.ds(n_y - REACH, REACH)),
                 y_send.at[r, 0], y_recv.at[r, 0, o], right_y),
            move(yb, (r, o, whole, pl.ds(n_y, REACH)), (r, o, whole, pl.ds(2 * n_y, REACH)),
                 y_send.at[r, 1], y_recv.at[r, 1, o], left_y),
        )

    def local_part(r, o):
        scale, back = ROUNDS[r]
        value = xb[r, o, own_x]
        result = scale * ((pot_ref[...] - (1.5 * COEF[0] + CENTRE)) * value)
        if r > 0:
            result = result - back * xb[r - 1, o, own_x]
        flat = value.reshape(n_x * n_y, n_z)
        along_z = jnp.zeros_like(flat)
        for k in range(1, REACH + 1):
            pair = pltpu.roll(flat, k, 1) + pltpu.roll(flat, n_z - k, 1)
            along_z = along_z + (-0.5 * COEF[k] * scale) * pair
        acc[o] = result + along_z.reshape(n_x, n_y, n_z)

    def halo_part(r, o):
        scale = ROUNDS[r][0]
        result = acc[o]
        for k in range(1, REACH + 1):
            pair = xb[r, o, pl.ds(REACH + k, n_x)] + xb[r, o, pl.ds(REACH - k, n_x)]
            pair = pair + yb[r, o, :, pl.ds(n_y + k, n_y)]
            pair = pair + yb[r, o, :, pl.ds(n_y - k, n_y)]
            result = result + (-0.5 * COEF[k] * scale) * pair
        return result

    half = n_band // 2

    def ring(direction, distance, source):
        width = n_x // 2 if distance == half else n_x
        block = every.at[source, pl.ds(direction * (n_x - width), width)]
        return pltpu.make_async_remote_copy(
            src_ref=block, dst_ref=block, send_sem=ring_send.at[direction, distance - 1],
            recv_sem=ring_recv.at[direction, distance - 1],
            device_id=device(band=peer("band", n_band - 1 if direction else 1)),
            device_id_type=MESH,
        )

    def source_at(direction, distance):
        return peer("band", distance if direction else n_band - distance)

    def pass_on(distance):
        for direction in (0, 1):
            source = source_at(direction, distance - 1)
            if distance > 1:
                ring(direction, distance - 1, source).wait_recv()
            ring(direction, distance, source).start()

    @pl.loop(0, n_orb)
    def _(o):
        for copy in halo(0, o):
            copy.start()

    greet(near, "band", 1)
    load_x.wait()
    load_y.wait()
    load_pot.wait()

    @pl.loop(0, n_orb)
    def _(o):
        local_part(0, o)

    depth = n_orb * n_y

    def rows_of(index):
        return pl.ds(pl.multiple_of(depth * index, depth), depth)

    def spread(target, o):
        start = pl.multiple_of(o * n_y, n_y)
        return pltpu.make_async_remote_copy(
            src_ref=every.at[band, target, pl.ds(start, n_y)],
            dst_ref=fc.at[pl.ds(pl.multiple_of(depth * band + start, n_y), n_y)],
            send_sem=a_send.at[target], recv_sem=a_recv.at[band],
            device_id=device(band=target), device_id_type=MESH,
        )

    def spread_whole(source, target):
        return pltpu.make_async_remote_copy(
            src_ref=every.at[band, target], dst_ref=fc.at[rows_of(source)],
            send_sem=a_send.at[target], recv_sem=a_recv.at[source],
            device_id=device(band=target), device_id_type=MESH,
        )

    def share(step, where, buf, send, recv):
        return pltpu.make_async_remote_copy(
            src_ref=buf.at[0], dst_ref=buf.at[step], send_sem=send.at[0],
            recv_sem=recv.at[step], device_id=device(**where(step)), device_id_type=MESH,
        )

    def sum_sent(steps, where, buf, send, recv):
        if steps:
            sent = buf.at[pl.ds(1, len(steps))]
            pltpu.make_async_remote_copy(
                src_ref=sent, dst_ref=sent, send_sem=send.at[0], recv_sem=recv.at[1],
                device_id=device(**where(steps[0])), device_id_type=MESH,
            ).wait_send()

    def by_distance(count):
        return sorted(range(1, count), key=lambda step: min(step, count - step))

    other_core = gy + 1 - 2 * lax.rem(gy, 2)
    band_steps = [0] + by_distance(n_band)
    phases = (
        (
            [2 * step + core for step in band_steps for core in (0, 1) if step + core > 0],
            lambda step: {
                "gy": other_core if step % 2 else gy, "band": peer("band", step // 2)
            },
            sums_band, band_send, band_recv,
        ),
        (
            by_distance(n_gy // 2),
            lambda step: {"gy": peer("gy", 2 * step)},
            sums_gy, gy_send, gy_recv,
        ),
        (
            by_distance(n_gx),
            lambda step: {"gx": peer("gx", step)},
            sums_gx, gx_send, gx_recv,
        ),
    )

    for r in range(3):
        if r == 1:
            pl.semaphore_wait(near, 2)
            greet(middle_way, "band", 2)
        if r == 2:
            pl.semaphore_wait(middle_way, 2)

        @pl.loop(0, n_orb)
        def _(o, r=r):
            for copy in halo(r, o):
                copy.wait_recv()
            result = halo_part(r, o)
            if r < 2:
                xb[r + 1, o, own_x] = result
                yb[r + 1, o, :, own_y] = result
                for copy in halo(r + 1, o):
                    copy.start()
            else:
                every[band, :, pl.ds(pl.multiple_of(o * n_y, n_y), n_y)] = result
                for step in reversed(by_distance(n_band)):
                    spread(peer("band", step), o).start()

        if r < 2:
            @pl.loop(0, n_orb)
            def _(o, r=r):
                local_part(r + 1, o)

    pass_on(1)
    if n_gx > 8:
        greet(far, "gx", 4)
    fc[rows_of(band)] = every[band, band]
    for step in by_distance(n_band):
        spread_whole(peer("band", step), band).wait_recv()

    parts = []
    for y in range(n_y):
        parts.append(split_two(fc[pl.ds(y, total, stride=n_y), :]))
    stacked = jnp.concatenate([jnp.concatenate(part, axis=0) for part in parts], axis=1)
    blocks = lax.dot_general(
        stacked, stacked, (((1,), (1,)), ((), ())), preferred_element_type=jnp.float32
    )
    blocks = blocks[:total] + blocks[total:]
    gram[:, : 2 * total] = blocks
    gram[:, 2 * total :] = jnp.zeros((total, n_z - 2 * total), jnp.float32)
    wide = gram[...]
    wide = wide + pltpu.roll(wide, n_z - total, 1)
    lane = lax.broadcasted_iota(jnp.int32, (8, n_z), 1)
    row = lax.broadcasted_iota(jnp.int32, (8, n_z), 0)
    groups = total // 8
    packed = jnp.where(lane < total, wide[:8], 0.0)
    for q in range(1, groups):
        moved = pltpu.roll(wide[8 * q : 8 * q + 8], total * q, 1)
        packed = jnp.where((lane >= total * q) & (lane < total * (q + 1)), moved, packed)

    def sum_sends(steps, where, value, buf, send, recv):
        buf[0] = value
        for step in reversed(steps):
            share(step, where, buf, send, recv).start()

    def sum_waits(steps, where, value, buf, send, recv):
        for step in steps:
            share(step, where, buf, send, recv).wait_recv()
            value = value + buf[step]
        return value

    second, third, first = phases
    if n_gx > 8:
        pl.semaphore_wait(far, 2)
    sum_sends(*first[:2], packed, *first[2:])
    pass_on(2)
    for r in range(3):
        for buf, send in ((xb.at[r, :, pl.ds(0, REACH)], x_send),
                          (yb.at[r, :, :, pl.ds(0, REACH if r else n_y)], y_send)):
            for direction in (0, 1):
                pltpu.make_async_remote_copy(
                    src_ref=buf, dst_ref=buf, send_sem=send.at[r, direction],
                    recv_sem=x_recv.at[0, 0, 0], device_id=device(gx=peer("gx", 1)),
                    device_id_type=MESH,
                ).wait_send()
    for step in by_distance(n_band):
        spread_whole(band, peer("band", step)).wait_send()
    for distance in range(3, half):
        pass_on(distance)
    packed = sum_waits(*first[:2], packed, *first[2:])
    sum_sends(*second[:2], packed, *second[2:])
    pass_on(half)
    sum_sent(*first)
    for direction in (0, 1):
        for distance in (1, 2):
            ring(direction, distance, source_at(direction, distance - 1)).wait_send()
    packed = sum_waits(*second[:2], packed, *second[2:])
    sum_sends(*third[:2], packed, *third[2:])
    sum_sent(*second)
    packed = sum_waits(*third[:2], packed, *third[2:])
    cells_all = float(n_x * n_y * n_z * n_gx * n_gy)
    packed = packed * (1.0 / cells_all)

    tiles = []
    for q in range(groups):
        tile = packed if q == 0 else pltpu.roll(packed, n_z - total * q, 1)
        eye = jnp.where(lax.rem(lane, total) == row + 8 * q, 1.0, 0.0)
        tiles.append(jnp.where(lane < total, tile, eye))
    for home in range(groups):
        columns = [
            [
                jnp.broadcast_to(tiles[q][:, 8 * home + at : 8 * home + at + 1], (8, n_z))
                for q in range(home, groups)
            ]
            for at in range(8)
        ]
        for at in range(8):
            pivot_row = jnp.broadcast_to(tiles[home][at : at + 1, :], (8, n_z))
            reciprocal = 1.0 / jnp.broadcast_to(columns[at][0][at : at + 1, :], (8, n_z))
            factors = [column * reciprocal for column in columns[at]]
            factors[0] = jnp.where(row > at, factors[0], 0.0)
            for factor, q in zip(factors, range(home, groups)):
                tiles[q] = tiles[q] - factor * pivot_row
            for later in range(at + 1, 8):
                value = jnp.broadcast_to(columns[later][0][at : at + 1, :], (8, n_z))
                columns[later] = [
                    column - factor * value for column, factor in zip(columns[later], factors)
                ]
    for q in range(groups):
        diagonal = jnp.sum(jnp.where(lane == row + 8 * q, tiles[q], 0.0), axis=1, keepdims=True)
        tiles[q] = jnp.where(lane < total, 0.0, tiles[q] * lax.rsqrt(diagonal))
    for q in range(groups):
        gram[pl.ds(8 * q, 8), :] = tiles[q]
    mine = gram[pl.ds(pl.multiple_of(8 * (band // 2), 8), 8), :]
    mine = jnp.where(lax.rem(band, 2) == 1, pltpu.roll(mine, 4, 0), mine)
    for direction in (0, 1):
        ring(direction, half, source_at(direction, half)).wait_recv()
    results = [[None] * n_x for _ in range(n_orb)]
    for j in range(total):
        source, o = j // n_orb, j % n_orb
        column = jnp.broadcast_to(mine[:, total + j : total + j + 1], (8, n_z))
        weights = [jnp.broadcast_to(column[i : i + 1, :], (8, n_z)) for i in range(n_orb)]
        for x in range(n_x):
            value = every[source, x, o * n_y : (o + 1) * n_y]
            for i in range(n_orb):
                term = weights[i] * value
                results[i][x] = term if j == 0 else results[i][x] + term
    for i in range(n_orb):
        for x in range(n_x):
            out_ref[i, x] = results[i][x]
    sum_sent(*third)
    for direction in (0, 1):
        for distance in range(3, half + 1):
            ring(direction, distance, source_at(direction, distance - 1)).wait_send()


def local(orbitals, potential, sizes):
    n_gx, n_gy, n_band = sizes
    n_orb, n_x, n_y, n_z = orbitals.shape
    total = n_orb * n_band
    f32 = jnp.float32
    dma = pltpu.SemaphoreType.DMA
    vmem = pl.BlockSpec(memory_space=pltpu.VMEM)
    return pl.pallas_call(
        functools.partial(kernel, sizes),
        out_shape=jax.ShapeDtypeStruct(orbitals.shape, f32),
        in_specs=[pl.BlockSpec(memory_space=pl.ANY)] * 2,
        out_specs=vmem,
        scratch_shapes=[
            pltpu.VMEM((n_x, n_y, n_z), f32),
            pltpu.VMEM((3, n_orb, n_x + 2 * REACH, n_y, n_z), f32),
            pltpu.VMEM((3, n_orb, n_x, 3 * n_y, n_z), f32),
            pltpu.VMEM((n_orb, n_x, n_y, n_z), f32),
            pltpu.VMEM((n_band, n_x, n_orb * n_y, n_z), f32),
            pltpu.VMEM((total * n_y, n_z), f32),
            pltpu.VMEM((n_gy // 2, 8, n_z), f32),
            pltpu.VMEM((2 * n_band, 8, n_z), f32),
            pltpu.VMEM((n_gx, 8, n_z), f32),
            pltpu.VMEM((total, n_z), f32),
            dma((3,)),
            dma((3, 2)), dma((3, 2, n_orb)), dma((3, 2)), dma((3, 2, n_orb)),
            dma((n_band,)), dma((n_band,)), dma((2, n_band // 2)), dma((2, n_band // 2)),
            dma((n_gy // 2,)), dma((n_gy // 2,)), dma((2 * n_band,)), dma((2 * n_band,)),
            dma((n_gx,)), dma((n_gx,)),
            *[pltpu.SemaphoreType.REGULAR] * 3,
        ],
        compiler_params=pltpu.CompilerParams(
            collective_id=0, has_side_effects=True, vmem_limit_bytes=32 * 1024 * 1024
        ),
        cost_estimate=pl.CostEstimate(
            flops=16_000_000, bytes_accessed=4 * 2 * orbitals.size, transcendentals=0
        ),
    )(
        pltpu.with_memory_space_constraint(orbitals, pltpu.HBM),
        pltpu.with_memory_space_constraint(potential, pltpu.HBM),
    )


def solution(mesh):
    sizes = tuple(mesh.shape[axis] for axis in ("gx", "gy", "band"))
    in_specs = (P("band", "gx", "gy", None), P("gx", "gy", None))
    out_specs = P("band", "gx", "gy", None)
    return jax.shard_map(
        functools.partial(local, sizes=sizes),
        mesh=mesh, in_specs=in_specs, out_specs=out_specs, check_vma=False,
    )
```
